256 devices in a mesh: dp: 16 (over z_hi, x, core), worker: 16 (over y, z_lo).
Axes of the slice: x: 4, y: 4, z: 8 (z_hi: 2, z_lo: 4; z = z_hi * 4 + z_lo), core: 2. Of those that a mesh axis runs over, the one named last changes fastest.
Arguments:
- activations: bfloat16 [3072, 4096], P('dp', 'worker'), may hold values from -12 to 12
- out_grads: bfloat16 [3072, 4096], P('dp', 'worker'), may hold values from -0.21875 to 0.21875
- old_input: float32 [4096, 4096], P('dp', 'worker'), may hold values from -1.5 to 1.5
- old_output: float32 [4096, 4096], P('dp', 'worker'), may hold values from -1.5 to 1.5
- input_basis: bfloat16 [4096, 4096], P('dp', 'worker'), may hold values from -0.09375 to 0.09375
- output_basis: bfloat16 [4096, 4096], P('worker', 'dp'), may hold values from -0.09375 to 0.09375
- input_eigen: float32 [4096], P('dp'), may hold values from 0.5 to 2
- output_eigen: float32 [4096], P('worker'), may hold values from 0.5 to 2
Outputs:
- input_factor: float32 [4096, 4096], P('dp', 'worker')
- output_factor: float32 [4096, 4096], P('dp', 'worker')
- preconditioned: float32 [4096, 4096], P('dp', 'worker')
The draws below stay inside these ranges and needn't reach their ends.
All inputs are finite; a program needn't handle non-finite values.
Results may differ from the reference program's by a relative error of at most 0.0059.
Values may be sent and summed in bfloat16 or wider, within the bound.
A program may use at most 64 MiB of HBM per device.

```python
import math
import jax
import jax.numpy as jnp

DIN = 4096
DOUT = 4096
TOKENS = 3072


def block_scale(stream_key, dims, split, least, largest):
    level, own = 1.0, jax.random.fold_in(stream_key, 6)
    for position, blocks in split:
        draws = jnp.exp(jax.random.uniform(jax.random.fold_in(own, position), (blocks,), jnp.float32, least / len(split), largest / len(split)))
        level = level * jnp.repeat(draws, dims[position] // blocks).reshape([-1 if axis == position else 1 for axis in range(len(dims))])
    return level


def bell_draw(stream_key, extent, scale, most, split=(), kind=jnp.bfloat16):
    loudness = block_scale(stream_key, extent, split, -0.22, 0.18) if split else 1.0
    values = jax.random.normal(stream_key, extent, jnp.float32) * scale * loudness
    return jnp.minimum(jnp.maximum(values, -most), most).astype(kind)


def setup_inputs(seed: int = 0) -> dict:
    arg_keys = jax.random.split(jax.random.key(seed), 9)
    return {
        "activations": bell_draw(arg_keys[0], (TOKENS, DIN), 2.0, 12.0, ((0, 16), (1, 16))),
        "out_grads": bell_draw(arg_keys[1], (TOKENS, DOUT), (TOKENS // 4) ** -0.5, 0.21875, ((0, 16), (1, 16))),
        "old_input": bell_draw(arg_keys[2], (DIN, DIN), 0.15, 1.5, ((0, 16), (1, 16)), jnp.float32),
        "old_output": bell_draw(arg_keys[3], (DOUT, DOUT), 0.15, 1.5, ((0, 16), (1, 16)), jnp.float32),
        "input_basis": bell_draw(arg_keys[4], (DIN, DIN), DIN ** -0.5, 0.09375, ((0, 16), (1, 16))),
        "output_basis": bell_draw(arg_keys[5], (DOUT, DOUT), DOUT ** -0.5, 0.09375, ((0, 16), (1, 16))),
        "input_eigen": jnp.clip(jnp.exp(math.log(2.0) - 1.3862944 * jax.random.uniform(arg_keys[6], (DIN,), jnp.float32) ** block_scale(arg_keys[6], (DIN,), ((0, 16),), -0.2, 0.2)), 0.5, 2.0),
        "output_eigen": jnp.clip(jnp.exp(math.log(2.0) - 1.3862944 * jax.random.uniform(arg_keys[7], (DOUT,), jnp.float32) ** block_scale(arg_keys[7], (DOUT,), ((0, 16),), -0.2, 0.2)), 0.5, 2.0),
    }


decay_rate = 0.8
damping = 0.1


def reference(activations, out_grads, old_input, old_output, input_basis, output_basis, input_eigen, output_eigen):
    a_gram = jnp.dot(activations.T, activations, preferred_element_type=jnp.float32)
    input_factor = decay_rate * old_input + ((1.0 - decay_rate) / TOKENS) * a_gram
    g_gram = jnp.dot(out_grads.T, out_grads, preferred_element_type=jnp.float32)
    output_factor = decay_rate * old_output + (1.0 - decay_rate) * g_gram
    gradient = jnp.dot(activations.T, out_grads, preferred_element_type=jnp.float32).astype(jnp.bfloat16)
    rotated = jnp.dot(input_basis.T, gradient, preferred_element_type=jnp.float32).astype(jnp.bfloat16)
    spectral = jnp.dot(rotated, output_basis, preferred_element_type=jnp.float32)
    scaled = (spectral / (input_eigen[:, None] * output_eigen[None, :] + damping)).astype(jnp.bfloat16)
    back = jnp.dot(input_basis, scaled, preferred_element_type=jnp.float32).astype(jnp.bfloat16)
    preconditioned = jnp.dot(back, output_basis.T, preferred_element_type=jnp.float32)
    return input_factor, output_factor, preconditioned
```

```python
import jax
import jax.numpy as jnp
from jax import lax
from jax.experimental import pallas as pl
from jax.experimental.pallas import tpu as pltpu
from jax.sharding import PartitionSpec as P

decay_rate = 0.8
damping = 0.1
BF = jnp.bfloat16
F32 = jnp.float32
MESH = pl.DeviceIdType.MESH
N = 16
contract_first = (((0,), (0,)), ((), ()))
contract_last = (((1,), (1,)), ((), ()))

A_ROW, G_COL, U_ROW, V_ROW, G_ROW, A_COL, SCALED, BACK = range(8)


def dot(a, b, dims=(((1,), (0,)), ((), ()))):
    return lax.dot_general(a, b, dims, preferred_element_type=F32)


def kernel(
    a_ref, g_ref, old_in_ref, old_out_ref, u_ref, v_ref, e_in_ref, e_out_ref,
    in_factor_ref, out_factor_ref, p_ref,
    a_row, g_col, u_row, v_row, g_row, a_col, sc, bk,
    u_sib, m_own, m_sib, r_part, r_x, r_z, r_zsend, s_part, s_y, s_z, s_zsend, acc, acc2,
    gs, gr, ps, pr, us, ur, ms, mr, rxs, rxr, rzs, rzr, sys_, syr, szs, szr,
):
    total_tokens = a_ref.shape[0] * N
    d = lax.axis_index("dp")
    w = lax.axis_index("worker")
    zh, x, c = d // 8, (d // 2) % 4, d % 2
    y, zl = w // 4, w % 4

    def dp_index(zh_, x_, c_):
        return (zh_ * 4 + x_) * 2 + c_

    def ring(v, j):
        return (v + j) % 4

    sibling = (dp_index(zh, x, 1 - c), w)
    opposite = (dp_index(1 - zh, x, c), w)

    def along_x(j):
        return (dp_index(zh, ring(x, j), c), w)

    def along_y(j):
        return (d, ring(y, j) * 4 + zl)

    def along_z(j):
        return (d, y * 4 + ring(zl, j))

    partner = (w, d)
    off_diagonal = d != w

    barrier = pltpu.get_barrier_semaphore()
    peers = [sibling, opposite]
    for j in (1, 2, 3):
        peers += [along_x(j), along_y(j), along_z(j)]
    for peer in peers:
        pl.semaphore_signal(barrier, inc=1, device_id=peer, device_id_type=MESH)

    @pl.when(off_diagonal)
    def _():
        pl.semaphore_signal(barrier, inc=1, device_id=partner, device_id_type=MESH)

    pl.semaphore_wait(barrier, len(peers) + off_diagonal.astype(jnp.int32))

    sent = []

    def send(src, dst, ssem, rsem, device):
        copy = pltpu.make_async_remote_copy(
            src_ref=src, dst_ref=dst, send_sem=ssem, recv_sem=rsem,
            device_id=device, device_id_type=MESH,
        )
        copy.start()
        sent.append(copy)

    def arrived(dst, rsem):
        pltpu.make_async_remote_copy(
            src_ref=dst, dst_ref=dst, send_sem=rsem, recv_sem=rsem,
            device_id=sibling, device_id_type=MESH,
        ).wait_recv()

    counts = [0] * 8
    bufs = [a_row, g_col, u_row, v_row, g_row, a_col, sc, bk]

    def push(op, slot, device, src=None):
        view = bufs[op].at[slot]
        send(view if src is None else src, view, gs.at[op, counts[op]], gr.at[op, slot], device)
        counts[op] += 1

    def got(op, slot):
        arrived(bufs[op].at[slot], gr.at[op, slot])

    def dp_start(op, src=None):
        push(op, d, opposite, src)
        for j in (1, 2, 3):
            push(op, d, along_x(j), src)
        push(op, d, sibling, src)

    def dp_opposite(op):
        slot = opposite[0]
        got(op, slot)
        for j in (1, 2, 3):
            push(op, slot, along_x(j))
        push(op, slot, sibling)

    def dp_share(op):
        for z_ in (zh, 1 - zh):
            for j in (1, 3, 2):
                slot = dp_index(z_, ring(x, j), c)
                got(op, slot)
                push(op, slot, sibling)

    def dp_finish(op):
        for z_ in (zh, 1 - zh):
            for j in (0, 1, 3, 2):
                got(op, dp_index(z_, ring(x, j), 1 - c))

    def wk_start(op, src=None):
        for j in (1, 2, 3):
            push(op, w, along_z(j), src)
        for j in (1, 3, 2):
            push(op, w, along_y(j), src)

    def wk_forward(op):
        for j in (1, 2, 3):
            slot = y * 4 + ring(zl, j)
            got(op, slot)
            for i in (1, 3, 2):
                push(op, slot, along_y(i))

    def wk_finish(op, each=None):
        for j in (0, 1, 2, 3):
            for i in (1, 3, 2):
                slot = ring(y, i) * 4 + ring(zl, j)
                got(op, slot)
                if each is not None:
                    each(slot)

    def turn_start(i, src, dst):
        copy = pltpu.make_async_remote_copy(
            src_ref=src, dst_ref=dst.at[d], send_sem=ps.at[i], recv_sem=pr.at[i],
            device_id=partner, device_id_type=MESH,
        )

        @pl.when(off_diagonal)
        def _():
            copy.start()

        @pl.when(jnp.logical_not(off_diagonal))
        def _():
            dst[w] = src[...]

    def turn_finish(i, src, dst):
        @pl.when(off_diagonal)
        def _():
            pltpu.make_async_remote_copy(
                src_ref=src, dst_ref=dst.at[w], send_sem=ps.at[i], recv_sem=pr.at[i],
                device_id=partner, device_id_type=MESH,
            ).wait()

    turn_start(0, a_ref, a_row)
    dp_start(G_COL, g_ref)
    wk_start(U_ROW, u_ref)
    g_col[d] = g_ref[...]
    u_row[w] = u_ref[...]
    turn_finish(0, a_ref, a_row)
    wk_start(A_ROW)
    turn_start(1, g_ref, g_row)
    dp_start(V_ROW, v_ref)
    v_row[d] = v_ref[...]
    dp_opposite(G_COL)
    wk_forward(U_ROW)
    wk_forward(A_ROW)
    dp_share(G_COL)
    dp_opposite(V_ROW)
    dp_start(A_COL, a_ref)
    a_col[d] = a_ref[...]
    dp_finish(G_COL)
    turn_finish(1, g_ref, g_row)

    def u_share(slot):
        pass

    wk_finish(U_ROW)
    for k in range(8):
        send(u_row.at[2 * k + 1 - c], u_sib.at[k], us.at[k], ur.at[k], sibling)
    wk_finish(A_ROW)

    def gram(left, right):
        acc[...] = jnp.zeros_like(acc)

        @pl.loop(0, N)
        def _(t):
            acc[...] += dot(left[t], right[t], contract_first)

    gram(g_col, a_row)
    m_own[...] = acc[...].astype(BF)
    send(m_own, m_sib, ms, mr, sibling)
    wk_start(G_ROW)
    dp_share(V_ROW)
    dp_opposite(A_COL)
    for k in range(8):
        arrived(u_sib.at[k], ur.at[k])
    arrived(m_sib, mr)

    def r_block(h, j):
        z_ = 1 - zh if h == 0 else zh
        k = z_ * 4 + ring(x, j)
        return dot(m_own[...], u_row[2 * k + c]) + dot(m_sib[...], u_sib[k])

    for h in (0, 1):
        for j in (2, 1, 3):
            r_part[h, j] = r_block(h, j).astype(BF)
            send(r_part.at[h, j], r_x.at[h, j], rxs.at[h, j], rxr.at[h, j], along_x(j))
    acc[...] = r_block(0, 0)
    acc2[...] = r_block(1, 0)
    for j in (1, 3, 2):
        arrived(r_x.at[0, j], rxr.at[0, j])
        acc[...] += r_x[0, j].astype(F32)
    r_zsend[...] = acc[...].astype(BF)
    send(r_zsend, r_z, rzs, rzr, opposite)
    wk_forward(G_ROW)
    for j in (1, 3, 2):
        arrived(r_x.at[1, j], rxr.at[1, j])
        acc2[...] += r_x[1, j].astype(F32)
    dp_finish(V_ROW)
    arrived(r_z, rzr)
    rotated = (acc2[...] + r_z[...].astype(F32)).T.astype(BF)

    def s_block(iy, iz):
        return dot(rotated, v_row[ring(y, iy) * 4 + ring(zl, iz)])

    for iz in (2, 1, 3, 0):
        for iy in (2, 1, 3):
            s_part[iy, iz] = s_block(iy, iz).astype(BF)
            send(s_part.at[iy, iz], s_y.at[iy, iz], sys_.at[iy, iz], syr.at[iy, iz], along_y(iy))
    dp_share(A_COL)
    for iz in (2, 1, 3, 0):
        acc[...] = s_block(0, iz)
        for iy in (1, 3, 2):
            arrived(s_y.at[iy, iz], syr.at[iy, iz])
            acc[...] += s_y[iy, iz].astype(F32)
        if iz:
            s_zsend[iz] = acc[...].astype(BF)
            send(s_zsend.at[iz], s_z.at[iz], szs.at[iz], szr.at[iz], along_z(iz))
    for iz in (1, 3, 2):
        arrived(s_z.at[iz], szr.at[iz])
        acc[...] += s_z[iz].astype(F32)
    scale = e_in_ref[...] * e_out_ref[...] + damping
    sc[d] = (acc[...] / scale).astype(BF)
    dp_start(SCALED)
    dp_opposite(SCALED)
    dp_share(SCALED)
    dp_finish(SCALED)

    acc[...] = jnp.zeros_like(acc)

    @pl.loop(0, N)
    def _(i):
        acc[...] += dot(u_row[i], sc[i])

    bk[w] = acc[...].astype(BF)
    wk_start(BACK)

    dp_finish(A_COL)
    gram(a_row, a_col)
    in_factor_ref[...] = decay_rate * old_in_ref[...] + ((1.0 - decay_rate) / total_tokens) * acc[...]
    wk_forward(BACK)
    wk_finish(G_ROW)
    gram(g_row, g_col)
    out_factor_ref[...] = decay_rate * old_out_ref[...] + (1.0 - decay_rate) * acc[...]

    wk_finish(BACK)
    acc[...] = jnp.zeros_like(acc)

    @pl.loop(0, N)
    def _(i):
        acc[...] += dot(bk[i], v_row[i], contract_last)

    p_ref[...] = acc[...]

    for copy in sent:
        copy.wait_send()


def body(activations, out_grads, old_input, old_output, input_basis, output_basis, input_eigen, output_eigen):
    tokens, feats = activations.shape
    block = (feats, feats)
    vmem = pl.BlockSpec(memory_space=pltpu.VMEM)
    dma = pltpu.SemaphoreType.DMA
    out = jax.ShapeDtypeStruct(block, F32)
    return pl.pallas_call(
        kernel,
        out_shape=(out, out, out),
        in_specs=[vmem] * 8,
        out_specs=(vmem, vmem, vmem),
        scratch_shapes=[
            pltpu.VMEM((N, tokens, feats), BF),
            pltpu.VMEM((N, tokens, feats), BF),
            pltpu.VMEM((N,) + block, BF),
            pltpu.VMEM((N,) + block, BF),
            pltpu.VMEM((N, tokens, feats), BF),
            pltpu.VMEM((N, tokens, feats), BF),
            pltpu.VMEM((N,) + block, BF),
            pltpu.VMEM((N,) + block, BF),
            pltpu.VMEM((8,) + block, BF),
            pltpu.VMEM(block, BF),
            pltpu.VMEM(block, BF),
            pltpu.VMEM((2, 4) + block, BF),
            pltpu.VMEM((2, 4) + block, BF),
            pltpu.VMEM(block, BF),
            pltpu.VMEM(block, BF),
            pltpu.VMEM((4, 4) + block, BF),
            pltpu.VMEM((4, 4) + block, BF),
            pltpu.VMEM((4,) + block, BF),
            pltpu.VMEM((4,) + block, BF),
            pltpu.VMEM(block, F32),
            pltpu.VMEM(block, F32),
            dma((8, N)), dma((8, N)),
            dma((2,)), dma((2,)),
            dma((8,)), dma((8,)),
            dma, dma,
            dma((2, 4)), dma((2, 4)),
            dma, dma,
            dma((4, 4)), dma((4, 4)),
            dma((4,)), dma((4,)),
        ],
        compiler_params=pltpu.CompilerParams(
            collective_id=0, has_side_effects=True, vmem_limit_bytes=48 << 20
        ),
        cost_estimate=pl.CostEstimate(flops=3_400_000_000, bytes_accessed=4 << 20, transcendentals=0),
        name="kfac",
    )(
        activations, out_grads, old_input, old_output, input_basis, output_basis,
        input_eigen[:, None], output_eigen[None, :],
    )


def solution(mesh):
    in_specs = (
        P("dp", "worker"),
        P("dp", "worker"),
        P("dp", "worker"),
        P("dp", "worker"),
        P("dp", "worker"),
        P("worker", "dp"),
        P("dp"),
        P("worker"),
    )
    out_specs = (P("dp", "worker"), P("dp", "worker"), P("dp", "worker"))
    return jax.shard_map(body, mesh=mesh, in_specs=in_specs, out_specs=out_specs, check_vma=False)
```

```python
import jax
import jax.numpy as jnp
from jax import lax
from jax.experimental import pallas as pl
from jax.experimental.pallas import tpu as pltpu
from jax.sharding import PartitionSpec as P

decay_rate = 0.8
damping = 0.1
BF = jnp.bfloat16
F32 = jnp.float32
MESH = pl.DeviceIdType.MESH
N = 16
contract_first = (((0,), (0,)), ((), ()))
contract_last = (((1,), (1,)), ((), ()))

A_ROW, G_COL, U_ROW, V_ROW, G_ROW, A_COL, BACK, BACK2 = range(8)


def dot(a, b, dims=(((1,), (0,)), ((), ()))):
    return lax.dot_general(a, b, dims, preferred_element_type=F32)


def kernel(
    a_ref, g_ref, old_in_ref, old_out_ref, u_ref, v_ref, e_in_ref, e_out_ref,
    in_factor_ref, out_factor_ref, p_ref,
    a_row, g_col, u_row, v_row, g_row, a_col, sc, bk, old,
    u_sib, m_own, w_f32, w_part, w_t, w_y, w_z, w_zsend, wt_own, wt_sib, r_part, r_x, r_z, r_zsend, r_f32,
    e_opp, e_own, acc, p_acc, scale,
    ls, gs, gr, ps, pr, xs, xr,
):
    total_tokens = a_ref.shape[0] * N
    d = lax.axis_index("dp")
    w = lax.axis_index("worker")
    zh, x, c = d // 8, (d // 2) % 4, d % 2
    y, zl = w // 4, w % 4

    def dp_at(r):
        return ((zh + r[0]) % 2 * 4 + (x + r[1]) % 4) * 2 + (c + r[2]) % 2

    def wk_at(r):
        return (y + r[0]) % 4 * 4 + (zl + r[1]) % 4

    def dp_dev(r):
        return (dp_at(r), w)

    def wk_dev(r):
        return (d, wk_at(r))

    partner = (w, d)
    off_diagonal = d != w
    SIB, OPP = (0, 0, 1), (1, 0, 0)

    local = [
        pltpu.make_async_copy(src, dst, ls.at[i])
        for i, (src, dst) in enumerate((
            (a_ref, a_col.at[d]), (u_ref, u_row.at[w]), (g_ref, g_col.at[d]), (v_ref, v_row.at[d]),
            (old_in_ref, old.at[0]), (old_out_ref, old.at[1]),
        ))
    ]
    for copy in local:
        copy.start()

    barrier = pltpu.get_barrier_semaphore()
    peers = [dp_dev(SIB), dp_dev(OPP)]
    for j in (1, 2, 3):
        peers += [dp_dev((0, j, 0)), wk_dev((j, 0)), wk_dev((0, j))]
    for peer in peers:
        pl.semaphore_signal(barrier, inc=1, device_id=peer, device_id_type=MESH)

    @pl.when(off_diagonal)
    def _():
        pl.semaphore_signal(barrier, inc=1, device_id=partner, device_id_type=MESH)

    pl.semaphore_wait(barrier, len(peers) + off_diagonal.astype(jnp.int32))

    sent = []
    pending = {}

    def send(src, dst, ssem, rsem, device, cond=None):
        copy = pltpu.make_async_remote_copy(
            src_ref=src, dst_ref=dst, send_sem=ssem, recv_sem=rsem,
            device_id=device, device_id_type=MESH,
        )
        if cond is None:
            copy.start()
        else:
            pl.when(cond)(copy.start)
        sent.append((copy, cond))

    def arrived(key):
        dst, rsem = pending.pop(key)
        pltpu.make_async_remote_copy(
            src_ref=dst, dst_ref=dst, send_sem=rsem, recv_sem=rsem,
            device_id=dp_dev(SIB), device_id_type=MESH,
        ).wait_recv()

    def message(key, src, dst, device, lands=None):
        i = len(messages)
        messages.append(key)
        send(src, dst, xs.at[i], xr.at[i], device)
        pending[key] = (dst if lands is None else lands, xr.at[i])

    messages = []
    counts = [0] * 8
    unsent = {}
    bufs = [a_row, g_col, u_row, v_row, g_row, a_col, bk.at[0], bk.at[1]]

    def push(op, slot, to):
        mirror = tuple((a - b) % n for a, b, n in zip(slot, to, (2, 4, 2)))
        i = (mirror[0] * 4 + mirror[1]) * 2 + mirror[2]
        view = bufs[op].at[dp_at(slot)]
        send(view, view, gs.at[op, counts[op]], gr.at[op, i], dp_dev(to))
        counts[op] += 1
        pending[op, mirror] = (bufs[op].at[dp_at(mirror)], gr.at[op, i])

    def got(op, slot):
        arrived((op, slot))

    def dp_start(op):
        push(op, (0, 0, 0), OPP)
        for j in (2, 1, 3):
            push(op, (0, 0, 0), (0, j, 0))
        push(op, (0, 0, 0), SIB)

    def dp_opposite(op):
        got(op, OPP)
        for j in (2, 1, 3):
            push(op, OPP, (0, j, 0))
        push(op, OPP, SIB)

    def dp_share(op):
        for z in (0, 1):
            for j in (1, 3, 2):
                got(op, (z, j, 0))
                push(op, (z, j, 0), SIB)

    def dp_finish(op):
        for z in (0, 1):
            for j in (0, 1, 3, 2):
                got(op, (z, j, 1))

    upper = zl >= 2
    middle = jnp.logical_or(zl == 1, zl == 2)

    def line(v):
        return jnp.where(upper, 3 - v, v)

    inner = line(jnp.where(middle, 2, 1))
    outer = line(0)
    z_order = (zl, line(jnp.where(middle, 0, 1)), line(2), line(3))

    def wk_slot(op, iy, n):
        return bufs[op].at[(y + iy) % 4 * 4 + z_order[n]]

    def wk_send(op, src, dst, i, device, cond=None):
        send(src, dst, gs.at[op, counts[op]], gr.at[op, i], device, cond)
        counts[op] += 1

    def wk_line(op, n, to, cond):
        view = wk_slot(op, 0, n)
        wk_send(op, view, view, 16 + z_order[n], (d, y * 4 + to), cond)

    def wk_both(op, n):
        for iy in (1, 3):
            view = wk_slot(op, 0, n)
            i = (4 - iy) * 4 + n
            wk_send(op, view, view, i, wk_dev((iy, 0)))
            pending[op, 4 - iy, n] = (wk_slot(op, 4 - iy, n), gr.at[op, i])

    def wk_start(op):
        wk_line(op, 0, inner, None)
        wk_line(op, 0, outer, middle)
        wk_both(op, 0)
        for n in (1, 2, 3):
            pending[op, 0, n] = (wk_slot(op, 0, n), gr.at[op, 16 + z_order[n]])
        unsent[op] = [1, 2, 3]

    def wk_forward(op, *ns):
        for n in ns:
            arrived((op, 0, n))
            wk_line(op, n, inner if n == 1 else outer, middle)
            wk_both(op, n)
            unsent[op].remove(n)

    def wk_cross(op, *ns):
        for n in ns:
            for h, iy in ((0, 3), (1, 1)):
                arrived((op, iy, n))
                size = bufs[op].shape[1] // 2
                rows = pl.ds(h * size, size)
                view = wk_slot(op, iy, n).at[rows]
                i = h * 8 + n
                wk_send(op, view, view, i, wk_dev((4 - iy, 0)))
                pending[op, 2, n, h] = (wk_slot(op, 2, n).at[rows], gr.at[op, i])

    def wk_finish(op, *ns):
        for n in ns:
            for h in (0, 1):
                arrived((op, 2, n, h))

    def turn(i, src, dst):
        return pltpu.make_async_remote_copy(
            src_ref=src.at[d], dst_ref=dst.at[d], send_sem=ps.at[i], recv_sem=pr.at[i],
            device_id=partner, device_id_type=MESH,
        )

    def turn_start(i, src, dst):
        @pl.when(off_diagonal)
        def _():
            turn(i, src, dst).start()

        @pl.when(jnp.logical_not(off_diagonal))
        def _():
            dst[w] = src[d]

    def turn_finish(i, src, dst):
        @pl.when(off_diagonal)
        def _():
            turn(i, src, dst).wait()

    def finish():
        for op in unsent:
            wk_forward(op, *unsent[op])
        for key in list(pending):
            arrived(key)
        for copy, cond in sent:
            if cond is None:
                copy.wait_send()
            else:
                pl.when(cond)(copy.wait_send)

    def gram(left, right, slots=None):
        if slots is None:
            acc[...] = jnp.zeros_like(acc)

        @pl.loop(0, N if slots is None else 4)
        def _(t):
            if slots is not None:
                t = slots(t)
            acc[...] += dot(left[t], right[t], contract_first)

    local[0].wait()
    turn_start(0, a_col, a_row)
    for copy in local[1:]:
        copy.wait()
    wk_start(U_ROW)
    dp_start(G_COL)
    e_own[...] = jnp.broadcast_to(e_in_ref[...], e_own.shape)
    message("e", e_own, e_opp, dp_dev(OPP))
    turn_finish(0, a_col, a_row)
    wk_start(A_ROW)
    dp_opposite(G_COL)
    dp_start(V_ROW)
    wk_cross(U_ROW, 0)
    wk_forward(A_ROW, 1)
    wk_cross(A_ROW, 0)
    wk_forward(A_ROW, 2)
    wk_cross(A_ROW, 1)
    dp_share(G_COL)
    wk_forward(A_ROW, 3)
    turn_start(1, g_col, g_row)
    wk_forward(U_ROW, 1)
    wk_cross(A_ROW, 2)
    dp_opposite(V_ROW)
    wk_cross(A_ROW, 3)
    wk_forward(U_ROW, 2)
    wk_cross(U_ROW, 1)
    arrived("e")
    column = jnp.broadcast_to(e_out_ref[...], acc.shape).T
    scale[0] = column * e_opp[0:1, :] + damping
    scale[1] = column * e_own[0:1, :] + damping
    dp_finish(G_COL)

    acc[...] = jnp.zeros_like(acc)
    for iy in (0, 1, 3):
        gram(a_row, g_col, lambda t, iy=iy: (y + iy) % 4 * 4 + t)
    wk_finish(A_ROW, 0, 1, 2, 3)
    gram(a_row, g_col, lambda t: (y + 2) % 4 * 4 + t)
    m_own[...] = acc[...].astype(BF)
    wk_forward(U_ROW, 3)
    dp_share(V_ROW)
    dp_finish(V_ROW)

    size = m_own.shape[0] // 2
    cols = [pl.ds(q * size, size) for q in (0, 1)]
    order = (2, 1, 3, 0)
    ways = ((0, 1), (1, 3))

    def w_block(iy, iz):
        return dot(m_own[...], v_row[wk_at((iy, iz))])

    def w_transit(q):
        for iz in order:
            for i, to in ways:
                message(("t", q, i, iz), w_part.at[q, 2, iz, cols[i]], w_t.at[q, i, iz], wk_dev((to, 0)))

    def w_along_y(q):
        for iz in order:
            for i, to in ways:
                arrived(("t", q, i, iz))
                w_part[q, to, iz] = w_f32[to, iz, :, cols[q]].astype(BF)
                w_part[q, to, iz, cols[i]] = (
                    w_f32[to, iz, cols[i], cols[q]] + w_t[q, i, iz].astype(F32)
                ).astype(BF)
                message(("y", q, i, iz), w_part.at[q, to, iz], w_y.at[q, i, iz], wk_dev((to, 0)))

    def w_along_z(q):
        for iz in order:
            for i, _ in ways:
                arrived(("y", q, i, iz))
            total = w_f32[0, iz, :, cols[q]] + w_y[q, 0, iz].astype(F32) + w_y[q, 1, iz].astype(F32)
            if iz:
                w_zsend[q, iz] = total.astype(BF)
                message(("z", q, iz), w_zsend.at[q, iz], w_z.at[q, iz], wk_dev((0, iz)))
            else:
                w_f32[0, 0, :, cols[q]] = total

    def w_done(q):
        for iz in (1, 3, 2):
            arrived(("z", q, iz))
        total = w_f32[0, 0, :, cols[q]]
        for iz in (1, 2, 3):
            total += w_z[q, iz].astype(F32)
        wt_own[q] = total.T.astype(BF)
        message(("w", q), wt_own.at[q], wt_sib.at[q], dp_dev(SIB))

    def r_block(q, h, j):
        k = (zh + 1 - h) % 2 * 4 + (x + j) % 4
        return dot(wt_own[q], u_row[2 * k + c]) + dot(wt_sib[q], u_sib[k])

    def r_along_x(q):
        arrived(("w", q))
        for j in (2, 1, 3):
            for h in (0, 1):
                r_part[q, j, h] = r_block(q, h, j).astype(BF)
            message(("r", q, j), r_part.at[q, j], r_x.at[q, j], dp_dev((0, j, 0)))
        for h in (0, 1):
            r_f32[q, h] = r_block(q, h, 0)

    def r_across(q):
        for j in (1, 3, 2):
            arrived(("r", q, j))
        for h in (0, 1):
            total = r_f32[q, h]
            for j in (1, 2, 3):
                total += r_x[q, j, h].astype(F32)
            r_f32[q, h] = total
            r_zsend[q, 1 - h] = total.astype(BF)
        message(("rz", q), r_zsend.at[q], r_z.at[q], dp_dev(OPP))

    def scaled_start(q):
        arrived(("rz", q))
        for h in (0, 1):
            spectral = r_f32[q, h] + r_z[q, h].astype(F32)
            sc[q, x, c, (zh + 1 - h) % 2] = (spectral / scale[h, cols[q], :]).astype(BF)
        own = sc.at[q, x, c]
        for j in (2, 1, 3):
            there = sc.at[q, (x + 4 - j) % 4, c]
            message(("sx", q, 4 - j), own, own, dp_dev((0, j, 0)), there)
        message(("sc", q, 0), own, own, dp_dev(SIB), sc.at[q, x, 1 - c])

    def scaled_share(q):
        for j in (1, 3, 2):
            arrived(("sx", q, j))
            view = sc.at[q, (x + j) % 4, c]
            message(("sc", q, j), view, view, dp_dev(SIB), sc.at[q, (x + j) % 4, 1 - c])

    def back(q):
        for j in (0, 1, 3, 2):
            arrived(("sc", q, j))
        acc[:, cols[0]] = jnp.zeros((2 * size, size), F32)

        @pl.loop(0, N)
        def _(i):
            acc[:, cols[0]] += dot(u_row[i], sc[q, (i // 2) % 4, i % 2, i // 8], contract_last)

        bk[q, w] = acc[:, cols[0]].astype(BF)
        wk_start(BACK + q)

    def project(q):
        @pl.loop(0, N)
        def _(i):
            p_acc[...] += dot(bk[q, i], v_row[i, :, cols[q]], contract_last)

    for iz in order:
        block = w_block(2, iz).astype(BF)
        for q in (0, 1):
            w_part[q, 2, iz] = block[:, q * size : (q + 1) * size]
    w_transit(0)
    w_transit(1)
    for iy in (1, 3, 0):
        for iz in order:
            w_f32[iy, iz] = w_block(iy, iz)
    w_along_y(0)
    wk_cross(U_ROW, 2)
    w_along_y(1)
    wk_cross(U_ROW, 3)
    dp_start(A_COL)
    w_along_z(0)
    wk_finish(U_ROW, 0, 1, 2, 3)
    for k in range(8):
        message(("u", k), u_row.at[2 * k + 1 - c], u_sib.at[k], dp_dev(SIB))
    w_done(0)
    w_along_z(1)
    for k in range(8):
        arrived(("u", k))
    r_along_x(0)
    turn_finish(1, g_col, g_row)
    wk_start(G_ROW)
    w_done(1)
    r_across(0)
    r_along_x(1)
    dp_opposite(A_COL)
    scaled_start(0)
    r_across(1)
    wk_forward(G_ROW, 1)
    scaled_share(0)
    scaled_start(1)
    wk_cross(G_ROW, 0)
    wk_forward(G_ROW, 2)
    back(0)
    scaled_share(1)
    wk_cross(G_ROW, 1)
    wk_forward(BACK, 1)
    wk_forward(G_ROW, 3)
    back(1)
    p_acc[...] = jnp.zeros_like(p_acc)
    wk_cross(BACK, 0)
    wk_forward(BACK, 2)
    wk_cross(G_ROW, 2)
    wk_forward(BACK2, 1)
    wk_cross(BACK, 1)
    wk_forward(BACK, 3)
    wk_cross(BACK2, 0)
    wk_forward(BACK2, 2)
    wk_cross(BACK, 2)
    dp_share(A_COL)
    wk_cross(G_ROW, 3)
    wk_forward(BACK2, 3)
    wk_cross(BACK, 3)
    wk_cross(BACK2, 1)

    dp_finish(A_COL)
    gram(a_row, a_col)
    in_factor_ref[...] = decay_rate * old[0] + ((1.0 - decay_rate) / total_tokens) * acc[...]
    wk_cross(BACK2, 2)
    wk_cross(BACK2, 3)
    wk_finish(G_ROW, 0, 1, 2, 3)
    gram(g_row, g_col)
    out_factor_ref[...] = decay_rate * old[1] + (1.0 - decay_rate) * acc[...]
    wk_finish(BACK, 0, 1, 2, 3)
    project(0)
    wk_finish(BACK2, 0, 1, 2, 3)
    project(1)
    p_ref[...] = p_acc[...]
    assert not pending
    finish()


def body(activations, out_grads, old_input, old_output, input_basis, output_basis, input_eigen, output_eigen):
    tokens, feats = activations.shape
    block = (feats, feats)
    low, thin, quarter = (feats // 2, feats), (feats, feats // 2), (feats // 2, feats // 2)
    vmem = pl.BlockSpec(memory_space=pltpu.VMEM)
    hbm = pl.BlockSpec(memory_space=pl.ANY)
    dma = pltpu.SemaphoreType.DMA
    out = jax.ShapeDtypeStruct(block, F32)
    return pl.pallas_call(
        kernel,
        out_shape=(out, out, out),
        in_specs=[hbm] * 6 + [vmem] * 2,
        out_specs=(vmem, vmem, vmem),
        scratch_shapes=[
            pltpu.VMEM((N, tokens, feats), BF),
            pltpu.VMEM((N, tokens, feats), BF),
            pltpu.VMEM((N,) + block, BF),
            pltpu.VMEM((N,) + block, BF),
            pltpu.VMEM((N, tokens, feats), BF),
            pltpu.VMEM((N, tokens, feats), BF),
            pltpu.VMEM((2, 4, 2, 2) + low, BF),
            pltpu.VMEM((2, N) + thin, BF),
            pltpu.VMEM((2,) + block, F32),
            pltpu.VMEM((8,) + block, BF),
            pltpu.VMEM(block, BF),
            pltpu.VMEM((4, 4) + block, F32),
            pltpu.VMEM((2, 4, 4) + thin, BF),
            pltpu.VMEM((2, 2, 4) + quarter, BF),
            pltpu.VMEM((2, 2, 4) + thin, BF),
            pltpu.VMEM((2, 4) + thin, BF),
            pltpu.VMEM((2, 4) + thin, BF),
            pltpu.VMEM((2,) + low, BF),
            pltpu.VMEM((2,) + low, BF),
            pltpu.VMEM((2, 4, 2) + low, BF),
            pltpu.VMEM((2, 4, 2) + low, BF),
            pltpu.VMEM((2, 2) + low, BF),
            pltpu.VMEM((2, 2) + low, BF),
            pltpu.VMEM((2, 2) + low, F32),
            pltpu.VMEM((8, feats), F32),
            pltpu.VMEM((8, feats), F32),
            pltpu.VMEM(block, F32),
            pltpu.VMEM(block, F32),
            pltpu.VMEM((2,) + block, F32),
            dma((6,)),
            dma((8, 24)), dma((8, 24)),
            dma((2,)), dma((2,)),
            dma((80,)), dma((80,)),
        ],
        compiler_params=pltpu.CompilerParams(
            collective_id=0, has_side_effects=True, vmem_limit_bytes=48 << 20
        ),
        cost_estimate=pl.CostEstimate(flops=3_400_000_000, bytes_accessed=4 << 20, transcendentals=0),
        name="kfac",
    )(
        activations, out_grads, old_input, old_output, input_basis, output_basis,
        input_eigen[None, :], output_eigen[None, :],
    )


def solution(mesh):
    in_specs = (
        P("dp", "worker"),
        P("dp", "worker"),
        P("dp", "worker"),
        P("dp", "worker"),
        P("dp", "worker"),
        P("worker", "dp"),
        P("dp"),
        P("worker"),
    )
    out_specs = (P("dp", "worker"), P("dp", "worker"), P("dp", "worker"))
    return jax.shard_map(body, mesh=mesh, in_specs=in_specs, out_specs=out_specs, check_vma=False)
```

```python
import jax
import jax.numpy as jnp
from jax import lax
from jax.experimental import pallas as pl
from jax.experimental.pallas import tpu as pltpu
from jax.sharding import PartitionSpec as P

decay_rate = 0.8
damping = 0.1
BF = jnp.bfloat16
F32 = jnp.float32
MESH = pl.DeviceIdType.MESH
N = 16
contract_first = (((0,), (0,)), ((), ()))
contract_last = (((1,), (1,)), ((), ()))

A_ROW, G_COL, U_ROW, V_ROW, G_ROW, A_COL, BACK, BACK2 = range(8)


def dot(a, b, dims=(((1,), (0,)), ((), ()))):
    return lax.dot_general(a, b, dims, preferred_element_type=F32)


def kernel(
    a_ref, g_ref, old_in_ref, old_out_ref, u_ref, v_ref, e_in_ref, e_out_ref,
    in_factor_ref, out_factor_ref, p_ref,
    a_row, g_col, u_row, v_row, g_row, a_col, sc, bk, old,
    u_sib, m_own, w_f32, w_part, w_t, w_y, w_z, w_zsend, wt_own, wt_sib, r_part, r_x, r_z, r_zsend, r_f32,
    e_opp, e_own, acc, p_acc, scale,
    ls, gs, gr, ps, pr, xs, xr,
):
    total_tokens = a_ref.shape[0] * N
    d = lax.axis_index("dp")
    w = lax.axis_index("worker")
    zh, x, c = d // 8, (d // 2) % 4, d % 2
    y, zl = w // 4, w % 4

    def dp_at(r):
        return ((zh + r[0]) % 2 * 4 + (x + r[1]) % 4) * 2 + (c + r[2]) % 2

    def wk_at(r):
        return (y + r[0]) % 4 * 4 + (zl + r[1]) % 4

    def dp_dev(r):
        return (dp_at(r), w)

    def wk_dev(r):
        return (d, wk_at(r))

    partner = (w, d)
    off_diagonal = d != w
    SIB, OPP = (0, 0, 1), (1, 0, 0)

    local = [
        pltpu.make_async_copy(src, dst, ls.at[i])
        for i, (src, dst) in enumerate((
            (a_ref, a_col.at[d]), (u_ref, u_row.at[w]), (g_ref, g_col.at[d]), (v_ref, v_row.at[d]),
            (old_in_ref, old.at[0]), (old_out_ref, old.at[1]),
        ))
    ]
    for copy in local:
        copy.start()

    barrier = pltpu.get_barrier_semaphore()
    peers = [dp_dev(SIB), dp_dev(OPP)]
    for j in (1, 2, 3):
        peers += [dp_dev((0, j, 0)), wk_dev((j, 0)), wk_dev((0, j))]
    for peer in peers:
        pl.semaphore_signal(barrier, inc=1, device_id=peer, device_id_type=MESH)

    @pl.when(off_diagonal)
    def _():
        pl.semaphore_signal(barrier, inc=1, device_id=partner, device_id_type=MESH)

    pl.semaphore_wait(barrier, len(peers) + off_diagonal.astype(jnp.int32))

    sent = []
    pending = {}

    def send(src, dst, ssem, rsem, device, cond=None):
        copy = pltpu.make_async_remote_copy(
            src_ref=src, dst_ref=dst, send_sem=ssem, recv_sem=rsem,
            device_id=device, device_id_type=MESH,
        )
        if cond is None:
            copy.start()
        else:
            pl.when(cond)(copy.start)
        sent.append((copy, cond))

    def arrived(key):
        dst, rsem = pending.pop(key)
        pltpu.make_async_remote_copy(
            src_ref=dst, dst_ref=dst, send_sem=rsem, recv_sem=rsem,
            device_id=dp_dev(SIB), device_id_type=MESH,
        ).wait_recv()

    def message(key, src, dst, device, lands=None):
        i = len(messages)
        messages.append(key)
        send(src, dst, xs.at[i], xr.at[i], device)
        pending[key] = (dst if lands is None else lands, xr.at[i])

    messages = []
    counts = [0] * 8
    unsent = {}
    chained = {}
    bufs = [a_row, g_col, u_row, v_row, g_row, a_col, bk.at[0], bk.at[1]]

    def push(op, slot, to):
        mirror = tuple((a - b) % n for a, b, n in zip(slot, to, (2, 4, 2)))
        i = (mirror[0] * 4 + mirror[1]) * 2 + mirror[2]
        view = bufs[op].at[dp_at(slot)]
        send(view, view, gs.at[op, counts[op]], gr.at[op, i], dp_dev(to))
        counts[op] += 1
        pending[op, mirror] = (bufs[op].at[dp_at(mirror)], gr.at[op, i])

    def got(op, slot):
        arrived((op, slot))

    def dp_start(op):
        push(op, (0, 0, 0), OPP)
        for j in (2, 1, 3):
            push(op, (0, 0, 0), (0, j, 0))
        push(op, (0, 0, 0), SIB)

    def dp_opposite(op):
        got(op, OPP)
        for j in (2, 1, 3):
            push(op, OPP, (0, j, 0))
        push(op, OPP, SIB)

    def dp_share(op):
        for z in (0, 1):
            for j in (1, 3, 2):
                got(op, (z, j, 0))
                push(op, (z, j, 0), SIB)

    def dp_finish(op):
        for z in (0, 1):
            for j in (0, 1, 3, 2):
                got(op, (z, j, 1))

    upper = zl >= 2
    middle = jnp.logical_or(zl == 1, zl == 2)

    def line(v):
        return jnp.where(upper, 3 - v, v)

    inner = line(jnp.where(middle, 2, 1))
    outer = line(0)
    z_order = (zl, line(jnp.where(middle, 0, 1)), line(2), line(3))

    def wk_slot(op, iy, n):
        return bufs[op].at[(y + iy) % 4 * 4 + z_order[n]]

    def wk_send(op, src, dst, i, device, cond=None):
        send(src, dst, gs.at[op, counts[op]], gr.at[op, i], device, cond)
        counts[op] += 1

    def wk_line(op, n, to, cond):
        view = wk_slot(op, 0, n)
        wk_send(op, view, view, 16 + z_order[n], (d, y * 4 + to), cond)

    def wk_both(op, n):
        for iy in (1, 3):
            view = wk_slot(op, 0, n)
            i = (4 - iy) * 4 + n
            wk_send(op, view, view, i, wk_dev((iy, 0)))
            pending[op, 4 - iy, n] = (wk_slot(op, 4 - iy, n), gr.at[op, i])

    def wk_start(op, along_y=True, direct=False):
        if direct:
            for n in (1, 2, 3):
                view = wk_slot(op, 0, 0)
                wk_send(op, view, view, 16 + zl, (d, y * 4 + z_order[n]))
        else:
            wk_line(op, 0, inner, None)
            wk_line(op, 0, outer, middle)
        for n in (1, 2, 3):
            pending[op, 0, n] = (wk_slot(op, 0, n), gr.at[op, 16 + z_order[n]])
        unsent[op] = [1, 2, 3]
        chained[op] = not direct
        if along_y:
            wk_both(op, 0)

    def wk_chain(op, *ns):
        for n in ns:
            arrived((op, 0, n))
            if chained[op]:
                wk_line(op, n, inner if n == 1 else outer, middle)
            unsent[op].remove(n)

    def wk_forward(op, *ns):
        for n in ns:
            wk_chain(op, n)
            wk_both(op, n)

    def wk_cross(op, *ns):
        for n in ns:
            for h, iy in ((0, 3), (1, 1)):
                arrived((op, iy, n))
                size = bufs[op].shape[1] // 2
                rows = pl.ds(h * size, size)
                view = wk_slot(op, iy, n).at[rows]
                i = h * 8 + n
                wk_send(op, view, view, i, wk_dev((4 - iy, 0)))
                pending[op, 2, n, h] = (wk_slot(op, 2, n).at[rows], gr.at[op, i])

    def wk_finish(op, *ns):
        for n in ns:
            for h in (0, 1):
                arrived((op, 2, n, h))

    def turn(i, src, dst):
        return pltpu.make_async_remote_copy(
            src_ref=src.at[d], dst_ref=dst.at[d], send_sem=ps.at[i], recv_sem=pr.at[i],
            device_id=partner, device_id_type=MESH,
        )

    def turn_start(i, src, dst):
        @pl.when(off_diagonal)
        def _():
            turn(i, src, dst).start()

        @pl.when(jnp.logical_not(off_diagonal))
        def _():
            dst[w] = src[d]

    def turn_finish(i, src, dst):
        @pl.when(off_diagonal)
        def _():
            turn(i, src, dst).wait()

    def finish():
        for op in unsent:
            wk_chain(op, *list(unsent[op]))
        for key in list(pending):
            arrived(key)
        for copy, cond in sent:
            if cond is None:
                copy.wait_send()
            else:
                pl.when(cond)(copy.wait_send)

    def gram(left, right, slots=None):
        if slots is None:
            acc[...] = jnp.zeros_like(acc)

        def four(first):
            acc[...] += sum(dot(left[first + t], right[first + t], contract_first) for t in range(4))

        if slots is not None:
            four(slots(0))
        else:
            pl.loop(0, N, step=4)(four)

    local[0].wait()
    turn_start(0, a_col, a_row)
    for copy in local[1:]:
        copy.wait()
    wk_start(U_ROW)
    dp_start(G_COL)
    e_own[...] = jnp.broadcast_to(e_in_ref[...], e_own.shape)
    message("e", e_own, e_opp, dp_dev(OPP))
    wk_forward(U_ROW, 1)
    wk_cross(U_ROW, 0)
    wk_chain(U_ROW, 2)
    turn_finish(0, a_col, a_row)
    wk_start(A_ROW)
    dp_opposite(G_COL)
    dp_start(V_ROW)
    wk_chain(U_ROW, 3)
    wk_forward(A_ROW, 1)
    wk_cross(A_ROW, 0)
    arrived("e")
    column = jnp.broadcast_to(e_out_ref[...], acc.shape).T
    scale[0] = column * e_opp[0:1, :] + damping
    scale[1] = column * e_own[0:1, :] + damping
    wk_forward(A_ROW, 2)
    wk_cross(A_ROW, 1)
    dp_share(G_COL)
    wk_forward(A_ROW, 3)
    turn_start(1, g_col, g_row)
    wk_both(U_ROW, 2)
    wk_cross(A_ROW, 2)
    dp_opposite(V_ROW)
    wk_cross(A_ROW, 3)
    wk_both(U_ROW, 3)
    dp_finish(G_COL)

    acc[...] = jnp.zeros_like(acc)
    for iy in (0, 1, 3):
        gram(a_row, g_col, lambda t, iy=iy: (y + iy) % 4 * 4 + t)
    wk_cross(U_ROW, 1)
    wk_finish(A_ROW, 0, 1, 2, 3)
    gram(a_row, g_col, lambda t: (y + 2) % 4 * 4 + t)
    m_own[...] = acc[...].astype(BF)
    dp_start(A_COL)
    dp_share(V_ROW)
    dp_finish(V_ROW)

    size = m_own.shape[0] // 2
    cols = [pl.ds(q * size, size) for q in (0, 1)]
    order = (2, 1, 3, 0)
    ways = ((0, 1), (1, 3))

    def w_block(iy, iz):
        return dot(m_own[...], v_row[wk_at((iy, iz))])

    def w_transit(q):
        for iz in order:
            for i, to in ways:
                message(("t", q, i, iz), w_part.at[q, 2, iz, cols[i]], w_t.at[q, i, iz], wk_dev((to, 0)))

    def w_along_y(q):
        for iz in order:
            for i, to in ways:
                arrived(("t", q, i, iz))
                w_part[q, to, iz] = w_f32[to, iz, :, cols[q]].astype(BF)
                w_part[q, to, iz, cols[i]] = (
                    w_f32[to, iz, cols[i], cols[q]] + w_t[q, i, iz].astype(F32)
                ).astype(BF)
                message(("y", q, i, iz), w_part.at[q, to, iz], w_y.at[q, i, iz], wk_dev((to, 0)))

    def w_along_z(q):
        for iz in order:
            for i, _ in ways:
                arrived(("y", q, i, iz))
            total = w_f32[0, iz, :, cols[q]] + w_y[q, 0, iz].astype(F32) + w_y[q, 1, iz].astype(F32)
            if iz:
                w_zsend[q, iz] = total.astype(BF)
                message(("z", q, iz), w_zsend.at[q, iz], w_z.at[q, iz], wk_dev((0, iz)))
            else:
                w_f32[0, 0, :, cols[q]] = total

    def w_done(q):
        for iz in (1, 3, 2):
            arrived(("z", q, iz))
        total = w_f32[0, 0, :, cols[q]]
        for iz in (1, 2, 3):
            total += w_z[q, iz].astype(F32)
        wt_own[q] = total.T.astype(BF)
        message(("w", q), wt_own.at[q], wt_sib.at[q], dp_dev(SIB))

    def r_block(q, h, j):
        k = (zh + 1 - h) % 2 * 4 + (x + j) % 4
        return dot(wt_own[q], u_row[2 * k + c]) + dot(wt_sib[q], u_sib[k])

    def r_along_x(q):
        arrived(("w", q))
        for j in (2, 1, 3):
            for h in (0, 1):
                r_part[q, j, h] = r_block(q, h, j).astype(BF)
            message(("r", q, j), r_part.at[q, j], r_x.at[q, j], dp_dev((0, j, 0)))
        for h in (0, 1):
            r_f32[q, h] = r_block(q, h, 0)

    def r_across(q):
        for j in (1, 3, 2):
            arrived(("r", q, j))
        for h in (0, 1):
            total = r_f32[q, h]
            for j in (1, 2, 3):
                total += r_x[q, j, h].astype(F32)
            r_f32[q, h] = total
            r_zsend[q, 1 - h] = total.astype(BF)
        message(("rz", q), r_zsend.at[q], r_z.at[q], dp_dev(OPP))

    def scaled_start(q):
        arrived(("rz", q))
        for h in (0, 1):
            spectral = r_f32[q, h] + r_z[q, h].astype(F32)
            sc[q, x, c, (zh + 1 - h) % 2] = (spectral / scale[h, cols[q], :]).astype(BF)
        own = sc.at[q, x, c]
        for j in (2, 1, 3):
            there = sc.at[q, (x + 4 - j) % 4, c]
            message(("sx", q, 4 - j), own, own, dp_dev((0, j, 0)), there)
        message(("sc", q, 0), own, own, dp_dev(SIB), sc.at[q, x, 1 - c])

    def scaled_share(q):
        for j in (1, 3, 2):
            arrived(("sx", q, j))
            view = sc.at[q, (x + j) % 4, c]
            message(("sc", q, j), view, view, dp_dev(SIB), sc.at[q, (x + j) % 4, 1 - c])

    def back(q):
        for j in (0, 1, 3, 2):
            arrived(("sc", q, j))
        total = jnp.zeros((2 * size, size), F32)
        for i in range(N):
            total += dot(u_row[i], sc[q, (i // 2) % 4, i % 2, i // 8], contract_last)
        bk[q, w] = total.astype(BF)
        wk_start(BACK + q, direct=True)

    def project(q):
        @pl.loop(0, N, step=4)
        def _(i):
            p_acc[...] += sum(dot(bk[q, i + t], v_row[i + t, :, cols[q]], contract_last) for t in range(4))

    for iz in order:
        block = w_block(2, iz).astype(BF)
        for q in (0, 1):
            w_part[q, 2, iz] = block[:, q * size : (q + 1) * size]
    w_transit(0)
    w_transit(1)
    for iy in (1, 3, 0):
        for iz in order:
            w_f32[iy, iz] = w_block(iy, iz)
    turn_finish(1, g_col, g_row)
    wk_start(G_ROW, along_y=False)
    w_along_y(0)
    wk_cross(U_ROW, 2, 3)
    w_along_y(1)
    wk_both(G_ROW, 0)
    dp_opposite(A_COL)
    w_along_z(0)
    wk_forward(G_ROW, 1)
    wk_finish(U_ROW, 0, 1, 2, 3)
    for k in range(8):
        message(("u", k), u_row.at[2 * k + 1 - c], u_sib.at[k], dp_dev(SIB))
    w_done(0)
    w_along_z(1)
    for k in range(8):
        arrived(("u", k))
    r_along_x(0)
    wk_forward(G_ROW, 2)
    w_done(1)
    wk_cross(G_ROW, 0)
    r_across(0)
    r_along_x(1)
    dp_share(A_COL)
    wk_forward(G_ROW, 3)
    wk_cross(G_ROW, 1)
    scaled_start(0)
    r_across(1)
    dp_finish(A_COL)

    gram(a_row, a_col)
    in_factor_ref[...] = decay_rate * old[0] + ((1.0 - decay_rate) / total_tokens) * acc[...]
    wk_cross(G_ROW, 2)
    scaled_share(0)
    scaled_start(1)
    wk_cross(G_ROW, 3)
    back(0)
    scaled_share(1)
    wk_cross(BACK, 0)
    wk_forward(BACK, 1)
    back(1)
    wk_forward(BACK, 2, 3)
    wk_cross(BACK, 1)
    wk_cross(BACK2, 0)
    wk_finish(G_ROW, 0, 1, 2, 3)
    gram(g_row, g_col)
    out_factor_ref[...] = decay_rate * old[1] + (1.0 - decay_rate) * acc[...]
    wk_cross(BACK, 2, 3)
    wk_forward(BACK2, 1, 2, 3)
    p_acc[...] = jnp.zeros_like(p_acc)
    wk_finish(BACK, 0, 1, 2, 3)
    wk_cross(BACK2, 1, 2)
    project(0)
    wk_cross(BACK2, 3)
    wk_finish(BACK2, 0, 1, 2, 3)
    project(1)
    p_ref[...] = p_acc[...]
    assert not pending
    finish()


def body(activations, out_grads, old_input, old_output, input_basis, output_basis, input_eigen, output_eigen):
    tokens, feats = activations.shape
    block = (feats, feats)
    low, thin, quarter = (feats // 2, feats), (feats, feats // 2), (feats // 2, feats // 2)
    vmem = pl.BlockSpec(memory_space=pltpu.VMEM)
    hbm = pl.BlockSpec(memory_space=pl.ANY)
    dma = pltpu.SemaphoreType.DMA
    out = jax.ShapeDtypeStruct(block, F32)
    return pl.pallas_call(
        kernel,
        out_shape=(out, out, out),
        in_specs=[hbm] * 6 + [vmem] * 2,
        out_specs=(vmem, vmem, vmem),
        scratch_shapes=[
            pltpu.VMEM((N, tokens, feats), BF),
            pltpu.VMEM((N, tokens, feats), BF),
            pltpu.VMEM((N,) + block, BF),
            pltpu.VMEM((N,) + block, BF),
            pltpu.VMEM((N, tokens, feats), BF),
            pltpu.VMEM((N, tokens, feats), BF),
            pltpu.VMEM((2, 4, 2, 2) + low, BF),
            pltpu.VMEM((2, N) + thin, BF),
            pltpu.VMEM((2,) + block, F32),
            pltpu.VMEM((8,) + block, BF),
            pltpu.VMEM(block, BF),
            pltpu.VMEM((4, 4) + block, F32),
            pltpu.VMEM((2, 4, 4) + thin, BF),
            pltpu.VMEM((2, 2, 4) + quarter, BF),
            pltpu.VMEM((2, 2, 4) + thin, BF),
            pltpu.VMEM((2, 4) + thin, BF),
            pltpu.VMEM((2, 4) + thin, BF),
            pltpu.VMEM((2,) + low, BF),
            pltpu.VMEM((2,) + low, BF),
            pltpu.VMEM((2, 4, 2) + low, BF),
            pltpu.VMEM((2, 4, 2) + low, BF),
            pltpu.VMEM((2, 2) + low, BF),
            pltpu.VMEM((2, 2) + low, BF),
            pltpu.VMEM((2, 2) + low, F32),
            pltpu.VMEM((8, feats), F32),
            pltpu.VMEM((8, feats), F32),
            pltpu.VMEM(block, F32),
            pltpu.VMEM(block, F32),
            pltpu.VMEM((2,) + block, F32),
            dma((6,)),
            dma((8, 24)), dma((8, 24)),
            dma((2,)), dma((2,)),
            dma((80,)), dma((80,)),
        ],
        compiler_params=pltpu.CompilerParams(
            collective_id=0, has_side_effects=True, vmem_limit_bytes=60 << 20
        ),
        cost_estimate=pl.CostEstimate(flops=3_400_000_000, bytes_accessed=4 << 20, transcendentals=0),
        name="kfac",
    )(
        activations, out_grads, old_input, old_output, input_basis, output_basis,
        input_eigen[None, :], output_eigen[None, :],
    )


def solution(mesh):
    in_specs = (
        P("dp", "worker"),
        P("dp", "worker"),
        P("dp", "worker"),
        P("dp", "worker"),
        P("dp", "worker"),
        P("worker", "dp"),
        P("dp"),
        P("worker"),
    )
    out_specs = (P("dp", "worker"), P("dp", "worker"), P("dp", "worker"))
    return jax.shard_map(body, mesh=mesh, in_specs=in_specs, out_specs=out_specs, check_vma=False)
```

```python
import jax
import jax.numpy as jnp
from jax import lax
from jax.experimental import pallas as pl
from jax.experimental.pallas import tpu as pltpu
from jax.sharding import PartitionSpec as P

decay_rate = 0.8
damping = 0.1
BF = jnp.bfloat16
F32 = jnp.float32
MESH = pl.DeviceIdType.MESH
N = 16
contract_first = (((0,), (0,)), ((), ()))
contract_last = (((1,), (1,)), ((), ()))

A_ROW, G_COL, U_ROW, V_ROW, G_ROW, A_COL, BACK, BACK2 = range(8)


def dot(a, b, dims=(((1,), (0,)), ((), ()))):
    return lax.dot_general(a, b, dims, preferred_element_type=F32)


def kernel(
    a_ref, g_ref, old_in_ref, old_out_ref, u_ref, v_ref, e_in_ref, e_out_ref,
    in_factor_ref, out_factor_ref, p_ref,
    a_row, g_col, u_row, v_row, g_row, a_col, sc, bk, old,
    u_sib, m_own, w_f32, w_part, w_t, w_y, w_z, w_zsend, wt_own, wt_sib, r_part, r_x, r_z, r_zsend, r_f32,
    e_opp, e_own, acc, p_acc, scale,
    ls, gs, gr, ps, pr, xs, xr,
):
    total_tokens = a_ref.shape[0] * N
    d = lax.axis_index("dp")
    w = lax.axis_index("worker")
    zh, x, c = d // 8, (d // 2) % 4, d % 2
    y, zl = w // 4, w % 4

    def dp_at(r):
        return ((zh + r[0]) % 2 * 4 + (x + r[1]) % 4) * 2 + (c + r[2]) % 2

    def wk_at(r):
        return (y + r[0]) % 4 * 4 + (zl + r[1]) % 4

    def dp_dev(r):
        return (dp_at(r), w)

    def wk_dev(r):
        return (d, wk_at(r))

    partner = (w, d)
    off_diagonal = d != w
    SIB, OPP = (0, 0, 1), (1, 0, 0)

    local = [
        pltpu.make_async_copy(src, dst, ls.at[i])
        for i, (src, dst) in enumerate((
            (a_ref, a_col.at[d]), (u_ref, u_row.at[w]), (g_ref, g_col.at[d]), (v_ref, v_row.at[d]),
            (old_in_ref, old.at[0]), (old_out_ref, old.at[1]),
        ))
    ]
    for copy in local:
        copy.start()

    barrier = pltpu.get_barrier_semaphore()
    peers = [dp_dev(SIB), dp_dev(OPP)]
    for j in (1, 2, 3):
        peers += [dp_dev((0, j, 0)), wk_dev((j, 0)), wk_dev((0, j))]
    for peer in peers:
        pl.semaphore_signal(barrier, inc=1, device_id=peer, device_id_type=MESH)

    @pl.when(off_diagonal)
    def _():
        pl.semaphore_signal(barrier, inc=1, device_id=partner, device_id_type=MESH)

    pl.semaphore_wait(barrier, len(peers) + off_diagonal.astype(jnp.int32))

    sent = []
    pending = {}

    def send(src, dst, ssem, rsem, device, cond=None):
        copy = pltpu.make_async_remote_copy(
            src_ref=src, dst_ref=dst, send_sem=ssem, recv_sem=rsem,
            device_id=device, device_id_type=MESH,
        )
        if cond is None:
            copy.start()
        else:
            pl.when(cond)(copy.start)
        sent.append((copy, cond))

    def arrived(key):
        dst, rsem = pending.pop(key)
        pltpu.make_async_remote_copy(
            src_ref=dst, dst_ref=dst, send_sem=rsem, recv_sem=rsem,
            device_id=dp_dev(SIB), device_id_type=MESH,
        ).wait_recv()

    def message(key, src, dst, device, lands=None):
        i = len(messages)
        messages.append(key)
        send(src, dst, xs.at[i], xr.at[i], device)
        pending[key] = (dst if lands is None else lands, xr.at[i])

    messages = []
    counts = [0] * 8
    unsent = {}
    chained = {}
    bufs = [a_row, g_col, u_row, v_row, g_row, a_col, bk.at[0], bk.at[1]]

    def push(op, slot, to):
        mirror = tuple((a - b) % n for a, b, n in zip(slot, to, (2, 4, 2)))
        i = (mirror[0] * 4 + mirror[1]) * 2 + mirror[2]
        view = bufs[op].at[dp_at(slot)]
        send(view, view, gs.at[op, counts[op]], gr.at[op, i], dp_dev(to))
        counts[op] += 1
        pending[op, mirror] = (bufs[op].at[dp_at(mirror)], gr.at[op, i])

    def got(op, slot):
        arrived((op, slot))

    def dp_start(op):
        push(op, (0, 0, 0), OPP)
        for j in (2, 1, 3):
            push(op, (0, 0, 0), (0, j, 0))
        push(op, (0, 0, 0), SIB)

    def dp_opposite(op):
        got(op, OPP)
        for j in (2, 1, 3):
            push(op, OPP, (0, j, 0))
        push(op, OPP, SIB)

    def dp_share(op):
        for z in (0, 1):
            for j in (1, 3, 2):
                got(op, (z, j, 0))
                push(op, (z, j, 0), SIB)

    def dp_finish(op):
        for z in (0, 1):
            for j in (0, 1, 3, 2):
                got(op, (z, j, 1))

    upper = zl >= 2
    middle = jnp.logical_or(zl == 1, zl == 2)

    def line(v):
        return jnp.where(upper, 3 - v, v)

    inner = line(jnp.where(middle, 2, 1))
    outer = line(0)
    z_order = (zl, line(jnp.where(middle, 0, 1)), line(2), line(3))

    def wk_slot(op, iy, n):
        return bufs[op].at[(y + iy) % 4 * 4 + z_order[n]]

    def wk_send(op, src, dst, i, device, cond=None):
        send(src, dst, gs.at[op, counts[op]], gr.at[op, i], device, cond)
        counts[op] += 1

    def wk_line(op, n, to, cond):
        view = wk_slot(op, 0, n)
        wk_send(op, view, view, 16 + z_order[n], (d, y * 4 + to), cond)

    def wk_both(op, n):
        for iy in (1, 3):
            view = wk_slot(op, 0, n)
            i = (4 - iy) * 4 + n
            wk_send(op, view, view, i, wk_dev((iy, 0)))
            pending[op, 4 - iy, n] = (wk_slot(op, 4 - iy, n), gr.at[op, i])

    def wk_start(op, along_y=True, direct=False):
        if direct:
            for n in (1, 2, 3):
                view = wk_slot(op, 0, 0)
                wk_send(op, view, view, 16 + zl, (d, y * 4 + z_order[n]))
        else:
            wk_line(op, 0, inner, None)
            wk_line(op, 0, outer, middle)
        for n in (1, 2, 3):
            pending[op, 0, n] = (wk_slot(op, 0, n), gr.at[op, 16 + z_order[n]])
        unsent[op] = [1, 2, 3]
        chained[op] = not direct
        if along_y:
            wk_both(op, 0)

    def wk_chain(op, *ns):
        for n in ns:
            arrived((op, 0, n))
            if chained[op]:
                wk_line(op, n, inner if n == 1 else outer, middle)
            unsent[op].remove(n)

    def wk_forward(op, *ns):
        for n in ns:
            wk_chain(op, n)
            wk_both(op, n)

    def wk_cross(op, *ns):
        for n in ns:
            for h, iy in ((0, 3), (1, 1)):
                arrived((op, iy, n))
                size = bufs[op].shape[1] // 2
                rows = pl.ds(h * size, size)
                view = wk_slot(op, iy, n).at[rows]
                i = h * 8 + n
                wk_send(op, view, view, i, wk_dev((4 - iy, 0)))
                pending[op, 2, n, h] = (wk_slot(op, 2, n).at[rows], gr.at[op, i])

    def wk_finish(op, *ns):
        for n in ns:
            for h in (0, 1):
                arrived((op, 2, n, h))

    def turn(i, src, dst):
        return pltpu.make_async_remote_copy(
            src_ref=src.at[d], dst_ref=dst.at[d], send_sem=ps.at[i], recv_sem=pr.at[i],
            device_id=partner, device_id_type=MESH,
        )

    def turn_start(i, src, dst):
        @pl.when(off_diagonal)
        def _():
            turn(i, src, dst).start()

        @pl.when(jnp.logical_not(off_diagonal))
        def _():
            dst[w] = src[d]

    def turn_finish(i, src, dst):
        @pl.when(off_diagonal)
        def _():
            turn(i, src, dst).wait()

    def finish():
        for op in unsent:
            wk_chain(op, *list(unsent[op]))
        for key in list(pending):
            arrived(key)
        for copy, cond in sent:
            if cond is None:
                copy.wait_send()
            else:
                pl.when(cond)(copy.wait_send)

    def gram(left, right, slots=None):
        if slots is None:
            acc[...] = jnp.zeros_like(acc)

        def four(first):
            acc[...] += sum(dot(left[first + t], right[first + t], contract_first) for t in range(4))

        if slots is not None:
            four(slots(0))
        else:
            pl.loop(0, N, step=4)(four)

    local[0].wait()
    turn_start(0, a_col, a_row)
    local[2].wait()
    dp_start(G_COL)
    local[1].wait()
    wk_start(U_ROW)
    for copy in local[3:]:
        copy.wait()
    dp_start(V_ROW)
    e_own[...] = jnp.broadcast_to(e_in_ref[...], e_own.shape)
    message("e", e_own, e_opp, dp_dev(OPP))
    wk_forward(U_ROW, 1)
    wk_cross(U_ROW, 0)
    dp_opposite(G_COL)
    turn_finish(0, a_col, a_row)
    wk_start(A_ROW)
    wk_chain(U_ROW, 2)
    wk_forward(A_ROW, 1)
    wk_cross(A_ROW, 0)
    arrived("e")
    column = jnp.broadcast_to(e_out_ref[...], acc.shape).T
    scale[0] = column * e_opp[0:1, :] + damping
    scale[1] = column * e_own[0:1, :] + damping
    wk_forward(A_ROW, 2)
    wk_chain(U_ROW, 3)
    wk_cross(A_ROW, 1)
    wk_forward(A_ROW, 3)
    turn_start(1, g_col, g_row)
    wk_both(U_ROW, 2)
    wk_cross(A_ROW, 2)
    dp_share(G_COL)
    wk_cross(A_ROW, 3)
    dp_opposite(V_ROW)
    wk_both(U_ROW, 3)
    dp_finish(G_COL)

    acc[...] = jnp.zeros_like(acc)
    for iy in (0, 1, 3):
        gram(a_row, g_col, lambda t, iy=iy: (y + iy) % 4 * 4 + t)
    wk_cross(U_ROW, 1)
    wk_finish(A_ROW, 0, 1, 2, 3)
    gram(a_row, g_col, lambda t: (y + 2) % 4 * 4 + t)
    m_own[...] = acc[...].astype(BF)
    dp_start(A_COL)
    dp_share(V_ROW)
    dp_finish(V_ROW)

    size = m_own.shape[0] // 2
    cols = [pl.ds(q * size, size) for q in (0, 1)]
    order = (2, 1, 3, 0)
    ways = ((0, 1), (1, 3))

    def w_block(iy, iz):
        return dot(m_own[...], v_row[wk_at((iy, iz))])

    def w_transit(q):
        for iz in order:
            for i, to in ways:
                message(("t", q, i, iz), w_part.at[q, 2, iz, cols[i]], w_t.at[q, i, iz], wk_dev((to, 0)))

    def w_along_y(q):
        for iz in order:
            for i, to in ways:
                arrived(("t", q, i, iz))
                w_part[q, to, iz] = w_f32[to, iz, :, cols[q]].astype(BF)
                w_part[q, to, iz, cols[i]] = (
                    w_f32[to, iz, cols[i], cols[q]] + w_t[q, i, iz].astype(F32)
                ).astype(BF)
                message(("y", q, i, iz), w_part.at[q, to, iz], w_y.at[q, i, iz], wk_dev((to, 0)))

    def w_along_z(q):
        for iz in order:
            for i, _ in ways:
                arrived(("y", q, i, iz))
            total = w_f32[0, iz, :, cols[q]] + w_y[q, 0, iz].astype(F32) + w_y[q, 1, iz].astype(F32)
            if iz:
                w_zsend[q, iz] = total.astype(BF)
                message(("z", q, iz), w_zsend.at[q, iz], w_z.at[q, iz], wk_dev((0, iz)))
            else:
                w_f32[0, 0, :, cols[q]] = total

    def w_done(q):
        for iz in (1, 3, 2):
            arrived(("z", q, iz))
        total = w_f32[0, 0, :, cols[q]]
        for iz in (1, 2, 3):
            total += w_z[q, iz].astype(F32)
        wt_own[q] = total.T.astype(BF)
        message(("w", q), wt_own.at[q], wt_sib.at[q], dp_dev(SIB))

    def r_block(q, h, j):
        k = (zh + 1 - h) % 2 * 4 + (x + j) % 4
        return dot(wt_own[q], u_row[2 * k + c]) + dot(wt_sib[q], u_sib[k])

    def r_along_x(q):
        arrived(("w", q))
        for j in (2, 1, 3):
            for h in (0, 1):
                r_part[q, j, h] = r_block(q, h, j).astype(BF)
            message(("r", q, j), r_part.at[q, j], r_x.at[q, j], dp_dev((0, j, 0)))
        for h in (0, 1):
            r_f32[q, h] = r_block(q, h, 0)

    def r_across(q):
        for j in (1, 3, 2):
            arrived(("r", q, j))
        for h in (0, 1):
            total = r_f32[q, h]
            for j in (1, 2, 3):
                total += r_x[q, j, h].astype(F32)
            r_f32[q, h] = total
            r_zsend[q, 1 - h] = total.astype(BF)
        message(("rz", q), r_zsend.at[q], r_z.at[q], dp_dev(OPP))

    def scaled_start(q):
        arrived(("rz", q))
        for h in (0, 1):
            spectral = r_f32[q, h] + r_z[q, h].astype(F32)
            sc[q, x, c, (zh + 1 - h) % 2] = (spectral / scale[h, cols[q], :]).astype(BF)
        own = sc.at[q, x, c]
        for j in (2, 1, 3):
            there = sc.at[q, (x + 4 - j) % 4, c]
            message(("sx", q, 4 - j), own, own, dp_dev((0, j, 0)), there)
        message(("sc", q, 0), own, own, dp_dev(SIB), sc.at[q, x, 1 - c])

    def scaled_share(q):
        for j in (1, 3, 2):
            arrived(("sx", q, j))
            view = sc.at[q, (x + j) % 4, c]
            message(("sc", q, j), view, view, dp_dev(SIB), sc.at[q, (x + j) % 4, 1 - c])

    def back(q):
        for j in (0, 1, 3, 2):
            arrived(("sc", q, j))
        total = jnp.zeros((2 * size, size), F32)
        for i in range(N):
            total += dot(u_row[i], sc[q, (i // 2) % 4, i % 2, i // 8], contract_last)
        bk[q, w] = total.astype(BF)
        wk_start(BACK + q, direct=True)

    def project(q):
        @pl.loop(0, N, step=4)
        def _(i):
            p_acc[...] += sum(dot(bk[q, i + t], v_row[i + t, :, cols[q]], contract_last) for t in range(4))

    for iz in order:
        block = w_block(2, iz).astype(BF)
        for q in (0, 1):
            w_part[q, 2, iz] = block[:, q * size : (q + 1) * size]
    w_transit(0)
    w_transit(1)
    for iy in (1, 3, 0):
        for iz in order:
            w_f32[iy, iz] = w_block(iy, iz)
    turn_finish(1, g_col, g_row)
    wk_start(G_ROW, along_y=False)
    w_along_y(0)
    wk_cross(U_ROW, 2, 3)
    w_along_y(1)
    wk_both(G_ROW, 0)
    dp_opposite(A_COL)
    w_along_z(0)
    wk_forward(G_ROW, 1)
    wk_finish(U_ROW, 0, 1, 2, 3)
    for k in range(8):
        message(("u", k), u_row.at[2 * k + 1 - c], u_sib.at[k], dp_dev(SIB))
    w_done(0)
    w_along_z(1)
    for k in range(8):
        arrived(("u", k))
    r_along_x(0)
    wk_forward(G_ROW, 2)
    w_done(1)
    wk_cross(G_ROW, 0)
    r_across(0)
    r_along_x(1)
    dp_share(A_COL)
    wk_forward(G_ROW, 3)
    wk_cross(G_ROW, 1)
    scaled_start(0)
    r_across(1)
    dp_finish(A_COL)

    gram(a_row, a_col)
    in_factor_ref[...] = decay_rate * old[0] + ((1.0 - decay_rate) / total_tokens) * acc[...]
    wk_cross(G_ROW, 2)
    scaled_share(0)
    scaled_start(1)
    wk_cross(G_ROW, 3)
    back(0)
    scaled_share(1)
    wk_cross(BACK, 0)
    wk_forward(BACK, 1)
    back(1)
    wk_forward(BACK, 2, 3)
    wk_cross(BACK, 1)
    wk_cross(BACK2, 0)
    wk_finish(G_ROW, 0, 1, 2, 3)
    gram(g_row, g_col)
    out_factor_ref[...] = decay_rate * old[1] + (1.0 - decay_rate) * acc[...]
    wk_cross(BACK, 2, 3)
    wk_forward(BACK2, 1, 2, 3)
    p_acc[...] = jnp.zeros_like(p_acc)
    wk_finish(BACK, 0, 1, 2, 3)
    wk_cross(BACK2, 1, 2)
    project(0)
    wk_cross(BACK2, 3)
    wk_finish(BACK2, 0, 1, 2, 3)
    project(1)
    p_ref[...] = p_acc[...]
    assert not pending
    finish()


def body(activations, out_grads, old_input, old_output, input_basis, output_basis, input_eigen, output_eigen):
    tokens, feats = activations.shape
    block = (feats, feats)
    low, thin, quarter = (feats // 2, feats), (feats, feats // 2), (feats // 2, feats // 2)
    vmem = pl.BlockSpec(memory_space=pltpu.VMEM)
    hbm = pl.BlockSpec(memory_space=pl.ANY)
    dma = pltpu.SemaphoreType.DMA
    out = jax.ShapeDtypeStruct(block, F32)
    return pl.pallas_call(
        kernel,
        out_shape=(out, out, out),
        in_specs=[hbm] * 6 + [vmem] * 2,
        out_specs=(vmem, vmem, vmem),
        scratch_shapes=[
            pltpu.VMEM((N, tokens, feats), BF),
            pltpu.VMEM((N, tokens, feats), BF),
            pltpu.VMEM((N,) + block, BF),
            pltpu.VMEM((N,) + block, BF),
            pltpu.VMEM((N, tokens, feats), BF),
            pltpu.VMEM((N, tokens, feats), BF),
            pltpu.VMEM((2, 4, 2, 2) + low, BF),
            pltpu.VMEM((2, N) + thin, BF),
            pltpu.VMEM((2,) + block, F32),
            pltpu.VMEM((8,) + block, BF),
            pltpu.VMEM(block, BF),
            pltpu.VMEM((4, 4) + block, F32),
            pltpu.VMEM((2, 4, 4) + thin, BF),
            pltpu.VMEM((2, 2, 4) + quarter, BF),
            pltpu.VMEM((2, 2, 4) + thin, BF),
            pltpu.VMEM((2, 4) + thin, BF),
            pltpu.VMEM((2, 4) + thin, BF),
            pltpu.VMEM((2,) + low, BF),
            pltpu.VMEM((2,) + low, BF),
            pltpu.VMEM((2, 4, 2) + low, BF),
            pltpu.VMEM((2, 4, 2) + low, BF),
            pltpu.VMEM((2, 2) + low, BF),
            pltpu.VMEM((2, 2) + low, BF),
            pltpu.VMEM((2, 2) + low, F32),
            pltpu.VMEM((8, feats), F32),
            pltpu.VMEM((8, feats), F32),
            pltpu.VMEM(block, F32),
            pltpu.VMEM(block, F32),
            pltpu.VMEM((2,) + block, F32),
            dma((6,)),
            dma((8, 24)), dma((8, 24)),
            dma((2,)), dma((2,)),
            dma((80,)), dma((80,)),
        ],
        compiler_params=pltpu.CompilerParams(
            collective_id=0, has_side_effects=True, vmem_limit_bytes=60 << 20
        ),
        cost_estimate=pl.CostEstimate(flops=3_400_000_000, bytes_accessed=4 << 20, transcendentals=0),
        name="kfac",
    )(
        activations, out_grads, old_input, old_output, input_basis, output_basis,
        input_eigen[None, :], output_eigen[None, :],
    )


def solution(mesh):
    in_specs = (
        P("dp", "worker"),
        P("dp", "worker"),
        P("dp", "worker"),
        P("dp", "worker"),
        P("dp", "worker"),
        P("worker", "dp"),
        P("dp"),
        P("worker"),
    )
    out_specs = (P("dp", "worker"), P("dp", "worker"), P("dp", "worker"))
    return jax.shard_map(body, mesh=mesh, in_specs=in_specs, out_specs=out_specs, check_vma=False)
```

```python
import jax
import jax.numpy as jnp
from jax import lax
from jax.experimental import pallas as pl
from jax.experimental.pallas import tpu as pltpu
from jax.sharding import PartitionSpec as P

decay_rate = 0.8
damping = 0.1
BF = jnp.bfloat16
F32 = jnp.float32
MESH = pl.DeviceIdType.MESH
N = 16
contract_first = (((0,), (0,)), ((), ()))
contract_last = (((1,), (1,)), ((), ()))

A_ROW, G_COL, U_ROW, V_ROW, G_ROW, A_COL, BACK, BACK2 = range(8)


def dot(a, b, dims=(((1,), (0,)), ((), ()))):
    return lax.dot_general(a, b, dims, preferred_element_type=F32)


def kernel(
    a_ref, g_ref, old_in_ref, old_out_ref, u_ref, v_ref, e_in_ref, e_out_ref,
    in_factor_ref, out_factor_ref, p_ref,
    a_row, g_col, u_row, v_row, g_row, a_col, sc, bk, old,
    u_sib, m_own, w_f32, w_part, w_t, w_y, w_z, w_zsend, wt_own, wt_sib, r_part, r_x, r_z, r_zsend, r_f32,
    e_opp, e_own, acc, p_acc, scale,
    ls, gs, gr, ps, pr, xs, xr,
):
    total_tokens = a_ref.shape[0] * N
    d = lax.axis_index("dp")
    w = lax.axis_index("worker")
    zh, x, c = d // 8, (d // 2) % 4, d % 2
    y, zl = w // 4, w % 4

    def dp_at(r):
        return ((zh + r[0]) % 2 * 4 + (x + r[1]) % 4) * 2 + (c + r[2]) % 2

    def wk_at(r):
        return (y + r[0]) % 4 * 4 + (zl + r[1]) % 4

    def dp_dev(r):
        return (dp_at(r), w)

    def wk_dev(r):
        return (d, wk_at(r))

    partner = (w, d)
    off_diagonal = d != w
    SIB, OPP = (0, 0, 1), (1, 0, 0)

    local = [
        pltpu.make_async_copy(src, dst, ls.at[i])
        for i, (src, dst) in enumerate((
            (a_ref, a_col.at[d]), (u_ref, u_row.at[w]), (g_ref, g_col.at[d]), (v_ref, v_row.at[d]),
            (old_in_ref, old.at[0]), (old_out_ref, old.at[1]),
        ))
    ]
    for copy in local:
        copy.start()

    barrier = pltpu.get_barrier_semaphore()
    peers = [dp_dev(SIB), dp_dev(OPP)]
    for j in (1, 2, 3):
        peers += [dp_dev((0, j, 0)), wk_dev((j, 0)), wk_dev((0, j))]
    for peer in peers:
        pl.semaphore_signal(barrier, inc=1, device_id=peer, device_id_type=MESH)

    @pl.when(off_diagonal)
    def _():
        pl.semaphore_signal(barrier, inc=1, device_id=partner, device_id_type=MESH)

    pl.semaphore_wait(barrier, len(peers) + off_diagonal.astype(jnp.int32))

    sent = []
    pending = {}

    def send(src, dst, ssem, rsem, device, cond=None):
        copy = pltpu.make_async_remote_copy(
            src_ref=src, dst_ref=dst, send_sem=ssem, recv_sem=rsem,
            device_id=device, device_id_type=MESH,
        )
        if cond is None:
            copy.start()
        else:
            pl.when(cond)(copy.start)
        sent.append((copy, cond))

    def arrived(key):
        dst, rsem = pending.pop(key)
        pltpu.make_async_remote_copy(
            src_ref=dst, dst_ref=dst, send_sem=rsem, recv_sem=rsem,
            device_id=dp_dev(SIB), device_id_type=MESH,
        ).wait_recv()

    def message(key, src, dst, device, lands=None):
        i = len(messages)
        messages.append(key)
        send(src, dst, xs.at[i], xr.at[i], device)
        pending[key] = (dst if lands is None else lands, xr.at[i])

    messages = []
    counts = [0] * 8
    unsent = {}
    chained = {}
    bufs = [a_row, g_col, u_row, v_row, g_row, a_col, bk.at[0], bk.at[1]]

    def push(op, slot, to):
        mirror = tuple((a - b) % n for a, b, n in zip(slot, to, (2, 4, 2)))
        i = (mirror[0] * 4 + mirror[1]) * 2 + mirror[2]
        view = bufs[op].at[dp_at(slot)]
        send(view, view, gs.at[op, counts[op]], gr.at[op, i], dp_dev(to))
        counts[op] += 1
        pending[op, mirror] = (bufs[op].at[dp_at(mirror)], gr.at[op, i])

    def got(op, slot):
        arrived((op, slot))

    def dp_start(op):
        push(op, (0, 0, 0), OPP)
        for j in (2, 1, 3):
            push(op, (0, 0, 0), (0, j, 0))
        push(op, (0, 0, 0), SIB)

    def dp_opposite(op):
        got(op, OPP)
        for j in (2, 1, 3):
            push(op, OPP, (0, j, 0))
        push(op, OPP, SIB)

    def dp_share(op):
        for z in (0, 1):
            for j in (1, 3, 2):
                got(op, (z, j, 0))
                push(op, (z, j, 0), SIB)

    def dp_finish(op):
        for z in (0, 1):
            for j in (0, 1, 3, 2):
                got(op, (z, j, 1))

    upper = zl >= 2
    middle = jnp.logical_or(zl == 1, zl == 2)

    def line(v):
        return jnp.where(upper, 3 - v, v)

    inner = line(jnp.where(middle, 2, 1))
    outer = line(0)
    z_order = (zl, line(jnp.where(middle, 0, 1)), line(2), line(3))

    def wk_slot(op, iy, n):
        return bufs[op].at[(y + iy) % 4 * 4 + z_order[n]]

    def wk_send(op, src, dst, i, device, cond=None):
        send(src, dst, gs.at[op, counts[op]], gr.at[op, i], device, cond)
        counts[op] += 1

    def wk_line(op, n, to, cond):
        view = wk_slot(op, 0, n)
        wk_send(op, view, view, 16 + z_order[n], (d, y * 4 + to), cond)

    def wk_both(op, n):
        for iy in (1, 3):
            view = wk_slot(op, 0, n)
            i = (4 - iy) * 4 + n
            wk_send(op, view, view, i, wk_dev((iy, 0)))
            pending[op, 4 - iy, n] = (wk_slot(op, 4 - iy, n), gr.at[op, i])

    def wk_start(op, along_y=True, direct=False):
        if direct:
            for n in (1, 2, 3):
                view = wk_slot(op, 0, 0)
                wk_send(op, view, view, 16 + zl, (d, y * 4 + z_order[n]))
        else:
            wk_line(op, 0, inner, None)
            wk_line(op, 0, outer, middle)
        for n in (1, 2, 3):
            pending[op, 0, n] = (wk_slot(op, 0, n), gr.at[op, 16 + z_order[n]])
        unsent[op] = [1, 2, 3]
        chained[op] = not direct
        if along_y:
            wk_both(op, 0)

    def wk_chain(op, *ns):
        for n in ns:
            arrived((op, 0, n))
            if chained[op]:
                wk_line(op, n, inner if n == 1 else outer, middle)
            unsent[op].remove(n)

    def wk_forward(op, *ns):
        for n in ns:
            wk_chain(op, n)
            wk_both(op, n)

    def wk_cross(op, *ns):
        for n in ns:
            for h, iy in ((0, 3), (1, 1)):
                arrived((op, iy, n))
                size = bufs[op].shape[1] // 2
                rows = pl.ds(h * size, size)
                view = wk_slot(op, iy, n).at[rows]
                i = h * 8 + n
                wk_send(op, view, view, i, wk_dev((4 - iy, 0)))
                pending[op, 2, n, h] = (wk_slot(op, 2, n).at[rows], gr.at[op, i])

    def wk_finish(op, *ns):
        for n in ns:
            for h in (0, 1):
                arrived((op, 2, n, h))

    def turn(i, src, dst):
        return pltpu.make_async_remote_copy(
            src_ref=src.at[d], dst_ref=dst.at[d], send_sem=ps.at[i], recv_sem=pr.at[i],
            device_id=partner, device_id_type=MESH,
        )

    def turn_start(i, src, dst):
        @pl.when(off_diagonal)
        def _():
            turn(i, src, dst).start()

        @pl.when(jnp.logical_not(off_diagonal))
        def _():
            dst[w] = src[d]

    def turn_finish(i, src, dst):
        @pl.when(off_diagonal)
        def _():
            turn(i, src, dst).wait()

    def finish():
        for op in unsent:
            wk_chain(op, *list(unsent[op]))
        for key in list(pending):
            arrived(key)
        for copy, cond in sent:
            if cond is None:
                copy.wait_send()
            else:
                pl.when(cond)(copy.wait_send)

    def gram(left, right, slots=None):
        if slots is None:
            acc[...] = jnp.zeros_like(acc)

        def four(first):
            acc[...] += sum(dot(left[first + t], right[first + t], contract_first) for t in range(4))

        if slots is not None:
            four(slots(0))
        else:
            pl.loop(0, N, step=4)(four)

    local[0].wait()
    turn_start(0, a_col, a_row)
    local[2].wait()
    dp_start(G_COL)
    local[1].wait()
    wk_start(U_ROW)
    for copy in local[3:]:
        copy.wait()
    dp_start(V_ROW)
    e_own[...] = jnp.broadcast_to(e_in_ref[...], e_own.shape)
    message("e", e_own, e_opp, dp_dev(OPP))
    wk_forward(U_ROW, 1)
    wk_cross(U_ROW, 0)
    dp_opposite(G_COL)
    turn_finish(0, a_col, a_row)
    wk_start(A_ROW)
    wk_chain(U_ROW, 2)
    wk_forward(A_ROW, 1)
    wk_cross(A_ROW, 0)
    arrived("e")
    column = jnp.broadcast_to(e_out_ref[...], acc.shape).T
    scale[0] = column * e_opp[0:1, :] + damping
    scale[1] = column * e_own[0:1, :] + damping
    wk_forward(A_ROW, 2)
    wk_chain(U_ROW, 3)
    wk_cross(A_ROW, 1)
    wk_forward(A_ROW, 3)
    turn_start(1, g_col, g_row)
    wk_both(U_ROW, 2)
    wk_cross(A_ROW, 2)
    dp_share(G_COL)
    wk_cross(A_ROW, 3)
    dp_opposite(V_ROW)
    wk_both(U_ROW, 3)
    dp_finish(G_COL)

    acc[...] = jnp.zeros_like(acc)
    for iy in (0, 1, 3):
        gram(a_row, g_col, lambda t, iy=iy: (y + iy) % 4 * 4 + t)
    wk_cross(U_ROW, 1)
    wk_finish(A_ROW, 0, 1, 2, 3)
    gram(a_row, g_col, lambda t: (y + 2) % 4 * 4 + t)
    m_own[...] = acc[...].astype(BF)
    dp_start(A_COL)
    dp_share(V_ROW)
    dp_finish(V_ROW)

    size = m_own.shape[0] // 2
    cols = [pl.ds(q * size, size) for q in (0, 1)]
    order = (2, 1, 3, 0)
    ways = ((0, 1), (1, 3))

    def w_block(iy, iz):
        return dot(m_own[...], v_row[wk_at((iy, iz))])

    def w_transit(q):
        for iz in order:
            for i, to in ways:
                message(("t", q, i, iz), w_part.at[q, 2, iz, cols[i]], w_t.at[q, i, iz], wk_dev((to, 0)))

    def w_along_y(q):
        for iz in order:
            for i, to in ways:
                arrived(("t", q, i, iz))
                w_part[q, to, iz] = w_f32[to, iz, :, cols[q]].astype(BF)
                w_part[q, to, iz, cols[i]] = (
                    w_f32[to, iz, cols[i], cols[q]] + w_t[q, i, iz].astype(F32)
                ).astype(BF)
                message(("y", q, i, iz), w_part.at[q, to, iz], w_y.at[q, i, iz], wk_dev((to, 0)))

    def w_along_z(q):
        for iz in order:
            for i, _ in ways:
                arrived(("y", q, i, iz))
            total = w_f32[0, iz, :, cols[q]] + w_y[q, 0, iz].astype(F32) + w_y[q, 1, iz].astype(F32)
            if iz:
                w_zsend[q, iz] = total.astype(BF)
                message(("z", q, iz), w_zsend.at[q, iz], w_z.at[q, iz], wk_dev((0, iz)))
            else:
                w_f32[0, 0, :, cols[q]] = total

    def w_done(q):
        for iz in (1, 3, 2):
            arrived(("z", q, iz))
        total = w_f32[0, 0, :, cols[q]]
        for iz in (1, 2, 3):
            total += w_z[q, iz].astype(F32)
        wt_own[q] = total.T.astype(BF)
        message(("w", q), wt_own.at[q], wt_sib.at[q], dp_dev(SIB))

    def r_block(q, h, j):
        k = (zh + 1 - h) % 2 * 4 + (x + j) % 4
        return dot(wt_own[q], u_row[2 * k + c]) + dot(wt_sib[q], u_sib[k])

    def r_along_x(q):
        arrived(("w", q))
        for j in (2, 1, 3):
            for h in (0, 1):
                r_part[q, j, h] = r_block(q, h, j).astype(BF)
            message(("r", q, j), r_part.at[q, j], r_x.at[q, j], dp_dev((0, j, 0)))
        for h in (0, 1):
            r_f32[q, h] = r_block(q, h, 0)

    def r_across(q):
        for j in (1, 3, 2):
            arrived(("r", q, j))
        for h in (0, 1):
            total = r_f32[q, h]
            for j in (1, 2, 3):
                total += r_x[q, j, h].astype(F32)
            r_f32[q, h] = total
            r_zsend[q, 1 - h] = total.astype(BF)
        message(("rz", q), r_zsend.at[q], r_z.at[q], dp_dev(OPP))

    def scaled_start(q):
        arrived(("rz", q))
        for h in (0, 1):
            spectral = r_f32[q, h] + r_z[q, h].astype(F32)
            sc[q, x, c, (zh + 1 - h) % 2] = (spectral / scale[h, cols[q], :]).astype(BF)
        own = sc.at[q, x, c]
        for j in (2, 1, 3):
            there = sc.at[q, (x + 4 - j) % 4, c]
            message(("sx", q, 4 - j), own, own, dp_dev((0, j, 0)), there)
        message(("sc", q, 0), own, own, dp_dev(SIB), sc.at[q, x, 1 - c])

    def scaled_share(q):
        for j in (1, 3, 2):
            arrived(("sx", q, j))
            view = sc.at[q, (x + j) % 4, c]
            message(("sc", q, j), view, view, dp_dev(SIB), sc.at[q, (x + j) % 4, 1 - c])

    def back(q):
        for j in (0, 1, 3, 2):
            arrived(("sc", q, j))
        total = jnp.zeros((2 * size, size), F32)
        for i in range(N):
            total += dot(u_row[i], sc[q, (i // 2) % 4, i % 2, i // 8], contract_last)
        bk[q, w] = total.astype(BF)
        wk_start(BACK + q, direct=True)

    def project(q):
        p_acc[...] += sum(dot(bk[q, i], v_row[i, :, cols[q]], contract_last) for i in range(N))

    for iz in order:
        block = w_block(2, iz).astype(BF)
        for q in (0, 1):
            w_part[q, 2, iz] = block[:, q * size : (q + 1) * size]
    w_transit(0)
    w_transit(1)
    for iy in (1, 3, 0):
        for iz in order:
            w_f32[iy, iz] = w_block(iy, iz)
    turn_finish(1, g_col, g_row)
    wk_start(G_ROW, along_y=False)
    w_along_y(0)
    wk_cross(U_ROW, 2, 3)
    w_along_y(1)
    wk_both(G_ROW, 0)
    dp_opposite(A_COL)
    w_along_z(0)
    wk_forward(G_ROW, 1)
    wk_finish(U_ROW, 0, 1, 2, 3)
    for k in range(8):
        message(("u", k), u_row.at[2 * k + 1 - c], u_sib.at[k], dp_dev(SIB))
    w_done(0)
    w_along_z(1)
    for k in range(8):
        arrived(("u", k))
    r_along_x(0)
    wk_forward(G_ROW, 2)
    w_done(1)
    wk_cross(G_ROW, 0)
    r_across(0)
    r_along_x(1)
    dp_share(A_COL)
    wk_forward(G_ROW, 3)
    wk_cross(G_ROW, 1)
    scaled_start(0)
    r_across(1)
    dp_finish(A_COL)

    gram(a_row, a_col)
    in_factor_ref[...] = decay_rate * old[0] + ((1.0 - decay_rate) / total_tokens) * acc[...]
    wk_cross(G_ROW, 2)
    scaled_share(0)
    scaled_start(1)
    wk_cross(G_ROW, 3)
    back(0)
    scaled_share(1)
    wk_cross(BACK, 0)
    wk_forward(BACK, 1)
    back(1)
    wk_forward(BACK, 2, 3)
    wk_cross(BACK, 1)
    wk_cross(BACK2, 0)
    wk_finish(G_ROW, 0, 1, 2, 3)
    gram(g_row, g_col)
    out_factor_ref[...] = decay_rate * old[1] + (1.0 - decay_rate) * acc[...]
    wk_cross(BACK, 2, 3)
    wk_forward(BACK2, 1, 2, 3)
    p_acc[...] = jnp.zeros_like(p_acc)
    wk_finish(BACK, 0, 1, 2, 3)
    wk_cross(BACK2, 1, 2)
    project(0)
    wk_cross(BACK2, 3)
    wk_finish(BACK2, 0, 1, 2, 3)
    project(1)
    p_ref[...] = p_acc[...]
    assert not pending
    finish()


def body(activations, out_grads, old_input, old_output, input_basis, output_basis, input_eigen, output_eigen):
    tokens, feats = activations.shape
    block = (feats, feats)
    low, thin, quarter = (feats // 2, feats), (feats, feats // 2), (feats // 2, feats // 2)
    vmem = pl.BlockSpec(memory_space=pltpu.VMEM)
    hbm = pl.BlockSpec(memory_space=pl.ANY)
    dma = pltpu.SemaphoreType.DMA
    out = jax.ShapeDtypeStruct(block, F32)
    return pl.pallas_call(
        kernel,
        out_shape=(out, out, out),
        in_specs=[hbm] * 6 + [vmem] * 2,
        out_specs=(vmem, vmem, vmem),
        scratch_shapes=[
            pltpu.VMEM((N, tokens, feats), BF),
            pltpu.VMEM((N, tokens, feats), BF),
            pltpu.VMEM((N,) + block, BF),
            pltpu.VMEM((N,) + block, BF),
            pltpu.VMEM((N, tokens, feats), BF),
            pltpu.VMEM((N, tokens, feats), BF),
            pltpu.VMEM((2, 4, 2, 2) + low, BF),
            pltpu.VMEM((2, N) + thin, BF),
            pltpu.VMEM((2,) + block, F32),
            pltpu.VMEM((8,) + block, BF),
            pltpu.VMEM(block, BF),
            pltpu.VMEM((4, 4) + block, F32),
            pltpu.VMEM((2, 4, 4) + thin, BF),
            pltpu.VMEM((2, 2, 4) + quarter, BF),
            pltpu.VMEM((2, 2, 4) + thin, BF),
            pltpu.VMEM((2, 4) + thin, BF),
            pltpu.VMEM((2, 4) + thin, BF),
            pltpu.VMEM((2,) + low, BF),
            pltpu.VMEM((2,) + low, BF),
            pltpu.VMEM((2, 4, 2) + low, BF),
            pltpu.VMEM((2, 4, 2) + low, BF),
            pltpu.VMEM((2, 2) + low, BF),
            pltpu.VMEM((2, 2) + low, BF),
            pltpu.VMEM((2, 2) + low, F32),
            pltpu.VMEM((8, feats), F32),
            pltpu.VMEM((8, feats), F32),
            pltpu.VMEM(block, F32),
            pltpu.VMEM(block, F32),
            pltpu.VMEM((2,) + block, F32),
            dma((6,)),
            dma((8, 24)), dma((8, 24)),
            dma((2,)), dma((2,)),
            dma((80,)), dma((80,)),
        ],
        compiler_params=pltpu.CompilerParams(
            collective_id=0, has_side_effects=True, vmem_limit_bytes=60 << 20
        ),
        cost_estimate=pl.CostEstimate(flops=3_400_000_000, bytes_accessed=4 << 20, transcendentals=0),
        name="kfac",
    )(
        activations, out_grads, old_input, old_output, input_basis, output_basis,
        input_eigen[None, :], output_eigen[None, :],
    )


def solution(mesh):
    in_specs = (
        P("dp", "worker"),
        P("dp", "worker"),
        P("dp", "worker"),
        P("dp", "worker"),
        P("dp", "worker"),
        P("worker", "dp"),
        P("dp"),
        P("worker"),
    )
    out_specs = (P("dp", "worker"), P("dp", "worker"), P("dp", "worker"))
    return jax.shard_map(body, mesh=mesh, in_specs=in_specs, out_specs=out_specs, check_vma=False)
```
